32 devices in a mesh: dp: 8 (over z, x), ctx: 4 (over y, core).
Axes of the slice: x: 2, y: 2, z: 4, core: 2. Of those that a mesh axis runs over, the one named last changes fastest.
Arguments:
- queries: bfloat16 [8, 896, 1024], P('dp', 'ctx'), may hold values from -5 to 5
- keys: bfloat16 [8, 896, 128], P('dp', 'ctx'), may hold values from -5 to 5
- values: bfloat16 [8, 896, 128], P('dp', 'ctx'), may hold values from -6 to 6
- out_grad: bfloat16 [8, 896, 1024], P('dp', 'ctx'), may hold values from -6 to 6
- segments: int32 [8, 896], P('dp', 'ctx'), may hold values from 0 to 2, never falling along the last dimension, each value on 1 to 672 neighbouring positions
- features: bfloat16 [8, 896, 8192], P('dp', 'ctx'), may hold values from -6 to 6
- projector: bfloat16 [8192, 512], P('dp'), may hold values from -0.25 to 0.25
- first_moment: float32 [512, 256], P(('dp', 'ctx')), may hold values from -10 to 10, as said below
- second_moment: float32 [512, 256], P(('dp', 'ctx')), may hold values from 0.01 to 100
- adam_step: int32 [1], replicated, may hold values from 10 to 1000
Outputs:
- query_grad: bfloat16 [8, 896, 1024], P('dp', 'ctx')
- update: float32 [8192, 256], P(('dp', 'ctx'))
- first_new: float32 [512, 256], P(('dp', 'ctx'))
- second_new: float32 [512, 256], P(('dp', 'ctx'))
The draws below stay inside these ranges and needn't reach their ends.
Inputs may be any that keep to these rules, and one draw needn't show every extreme that they name: `segments`: segment numbers never fall along a sequence; a document holds 1 to 672 tokens and one holds exactly that many. `first_moment`: each entry's magnitude is at most the square root of the same entry of second_moment.
All inputs are finite; a program needn't handle non-finite values.
Results may differ from the reference program's by a relative error of at most 0.0044.
The reference program's roundings to bfloat16 on the way (of `dscore`, `probs_low` and `kv_grad`) count: a program that leaves them out, or rounds other values in their place, can miss the bound.
Values may be sent and summed in bfloat16 or wider, within the bound.
A program may use at most 64 MiB of HBM per device.

```python
import math
import jax
import jax.numpy as jnp
import numpy as np
from jax import lax

D = 8192
HEADS = 8
HD = 128
RANK = 512
QW = 1024
KVW = 256
SEQ = 896
BATCH = 8


SHARP = 5.0


def moment_pair(key):
    base = jax.random.fold_in(key, 5)
    spread = jax.random.uniform(jax.random.fold_in(base, 1), (RANK, KVW), jnp.float32, math.log(0.01), math.log(100.0))
    second_values = jnp.exp(spread)
    ratio = jax.random.uniform(jax.random.fold_in(base, 2), (RANK, KVW), jnp.float32, -1.0, 1.0)
    return (ratio * jnp.sqrt(second_values), second_values)


def draw_queries(key, part):
    values_now = jnp.clip(jax.random.normal(jax.random.fold_in(key, 11), (BATCH, SEQ, QW), jnp.float32), -SHARP, SHARP)
    return values_now.astype(jnp.bfloat16)


def draw_keys(key, part):
    values_now = jnp.clip(jax.random.normal(jax.random.fold_in(key, 13), (BATCH, SEQ, HD), jnp.float32), -SHARP, SHARP)
    return values_now.astype(jnp.bfloat16)


def draw_first_moment(key, part):
    first_values, second_values = moment_pair(key)
    return first_values


def draw_second_moment(key, part):
    first_values, second_values = moment_pair(key)
    return second_values


def shard_levels(stream_key, extent, pieces, smallest, top_value):
    gain, own = 1.0, jax.random.fold_in(stream_key, 6)
    for position, blocks in pieces:
        heights = jnp.exp(jax.random.uniform(jax.random.fold_in(own, position), (blocks,), jnp.float32, smallest / len(pieces), top_value / len(pieces)))
        gain = gain * jnp.repeat(heights, extent[position] // blocks).reshape([-1 if axis == position else 1 for axis in range(len(extent))])
    return gain


def profile(number_of, total, most, lean):
    weights = [(1 << 20) // math.isqrt(standing ** lean) + 1 for standing in range(2, number_of + 1)]
    rest, counts = total - most - (number_of - 1), [1] * (number_of - 1)
    while rest > 0:
        candidates = [i for i in range(number_of - 1) if counts[i] < most]
        whole, left = sum([weights[i] for i in candidates]), rest
        for i in candidates:
            extra = min(most - counts[i], max(1, left * weights[i] // whole), rest)
            counts[i] = counts[i] + extra
            rest = rest - extra
    return np.array([most] + counts)


def ragged(stream_key, number_of, total, reach, slope):
    if number_of == 2:
        one = jax.random.randint(stream_key, (), max(1, total - reach), min(reach, total - 1) + 1)
        return jnp.stack([one, total - one])
    lengths = jnp.asarray(profile(number_of, total, reach, slope), jnp.int32)
    pairs = (number_of - 1) // 2
    source_of, sink = lengths[1:1 + 2 * pairs:2], lengths[2:2 + 2 * pairs:2]
    margin = jnp.minimum(source_of - 1, reach - sink)
    shifted = jax.random.randint(jax.random.fold_in(stream_key, 1), (pairs,), 0, 1 << 20) % (margin + 1)
    lengths = lengths.at[1:1 + 2 * pairs:2].set(source_of - shifted).at[2:2 + 2 * pairs:2].set(sink + shifted)
    return lengths[jax.random.permutation(jax.random.fold_in(stream_key, 2), number_of)]


def bell_draw(stream_key, shape, deviation, most, pieces=(), held_as=jnp.bfloat16):
    entries = jax.random.normal(stream_key, shape, jnp.float32) * deviation
    if len(pieces) > 0:
        entries = shard_levels(stream_key, shape, pieces, -0.22, 0.18) * entries
    return jnp.clip(entries, min=-most, max=most).astype(held_as)


def setup_inputs(seed: int = 0) -> dict:
    key_of = jax.random.split(jax.random.key(seed), 11)
    queries = draw_queries(jax.random.fold_in(key_of[10], 71), 0)
    keys = draw_keys(jax.random.fold_in(key_of[10], 71), 0)
    values = bell_draw(key_of[2], (BATCH, SEQ, HD), 1.0, 6.0, ((0, 8), (1, 4)))
    out_grad = bell_draw(key_of[3], (BATCH, SEQ, QW), 1.0, 6.0, ((0, 8), (1, 4)))
    segments = jax.vmap(lambda own: jnp.searchsorted(jnp.cumsum(ragged(own, 3, SEQ, 3 * SEQ // 4, 0)), jnp.arange(SEQ), side="right"))(jax.random.split(key_of[4], BATCH)).reshape((BATCH, SEQ)).astype(jnp.int32)
    features = bell_draw(key_of[5], (BATCH, SEQ, D), 1.0, 6.0, ((0, 8), (1, 4)))
    projector = bell_draw(key_of[6], (D, RANK), RANK ** -0.5, 0.25, ((0, 8),))
    first_moment = draw_first_moment(jax.random.fold_in(key_of[10], 71), 0)
    second_moment = draw_second_moment(jax.random.fold_in(key_of[10], 71), 0)
    adam_step = jax.random.randint(key_of[9], (1,), 10, 1001).astype(jnp.int32)
    return dict(queries=queries, keys=keys, values=values, out_grad=out_grad, segments=segments, features=features, projector=projector, first_moment=first_moment, second_moment=second_moment, adam_step=adam_step)


BETA_ONE = 0.9
BETA_TWO = 0.999
EPSILON = 1e-08

def group_backward(queries_g, keys_g, values_g, grads_g, segments_g):
    seq_len = queries_g.shape[0]
    scale = 1.0 / math.sqrt(HD)
    positions = jnp.arange(seq_len, dtype=jnp.int32)
    allowed = (positions[None, :] <= positions[:, None]) & (segments_g[None, :] == segments_g[:, None])
    query_heads = jnp.transpose(queries_g.reshape(seq_len, HEADS, HD), (1, 0, 2))
    grad_heads = jnp.transpose(grads_g.reshape(seq_len, HEADS, HD), (1, 0, 2))

    def one_head(pair):
        query_one, grad_one = pair
        scores = jnp.dot(query_one, keys_g.T, preferred_element_type=jnp.float32) * scale
        masked = jnp.where(allowed, scores, -jnp.inf)
        row_top = lax.optimization_barrier(jnp.max(masked, axis=1, keepdims=True))
        log_total = row_top + jnp.log(lax.optimization_barrier(jnp.sum(jnp.exp(masked - row_top), axis=1, keepdims=True)))
        probs = jnp.where(allowed, jnp.exp(masked - log_total), 0.0)
        dprob = jnp.dot(grad_one, values_g.T, preferred_element_type=jnp.float32)
        delta = lax.optimization_barrier(jnp.sum(probs * dprob, axis=1, keepdims=True))
        dscore = (probs * (dprob - delta)).astype(jnp.bfloat16)
        probs_low = probs.astype(jnp.bfloat16)
        query_part = (jnp.dot(dscore, keys_g, preferred_element_type=jnp.float32) * scale).astype(jnp.bfloat16)
        key_part = jnp.dot(dscore.T, query_one, preferred_element_type=jnp.float32) * scale
        value_part = jnp.dot(probs_low.T, grad_one, preferred_element_type=jnp.float32)
        return (query_part, key_part, value_part)
    query_part, key_part, value_part = lax.map(one_head, (query_heads, grad_heads))
    query_grad = jnp.transpose(query_part, (1, 0, 2)).reshape(seq_len, HEADS * HD)
    kv_grad = jnp.concatenate([lax.optimization_barrier(jnp.sum(key_part, axis=0)), lax.optimization_barrier(jnp.sum(value_part, axis=0))], axis=1).astype(jnp.bfloat16)
    return (query_grad, kv_grad)

def reference(queries, keys, values, out_grad, segments, features, projector, first_moment, second_moment, adam_step):

    def per_group(grad_total, items):
        queries_g, keys_g, values_g, grads_g, segments_g, features_g = items
        query_grad, kv_grad = group_backward(queries_g, keys_g, values_g, grads_g, segments_g)
        grad_total = grad_total + jnp.dot(features_g.T, kv_grad, preferred_element_type=jnp.float32)
        return (grad_total, query_grad)
    weight_grad, query_grad = lax.scan(per_group, jnp.zeros((D, 2 * HD), jnp.float32), (queries, keys, values, out_grad, segments, features))
    projector_wide = projector.astype(jnp.float32)
    projected = jnp.dot(projector_wide.T, weight_grad, precision=lax.Precision.HIGHEST)
    first_new = BETA_ONE * first_moment + (1.0 - BETA_ONE) * projected
    second_new = BETA_TWO * second_moment + (1.0 - BETA_TWO) * projected * projected
    step_count = adam_step[0].astype(jnp.float32)
    bias_first = 1.0 - jnp.power(jnp.float32(BETA_ONE), step_count)
    bias_second = 1.0 - jnp.power(jnp.float32(BETA_TWO), step_count)
    direction = first_new / bias_first / (jnp.sqrt(second_new / bias_second) + EPSILON)
    update = jnp.dot(projector_wide, direction, precision=lax.Precision.HIGHEST)
    return (query_grad, update, first_new, second_new)
```

```python
import functools
import math

import jax
import jax.numpy as jnp
from jax import lax
from jax.experimental import pallas as pl
from jax.experimental.pallas import tpu as pltpu
from jax.sharding import PartitionSpec as P

HEADS = 8
BETA_ONE = 0.9
BETA_TWO = 0.999
EPSILON = 1e-08
MESH = pl.DeviceIdType.MESH
F32 = jnp.float32
BF16 = jnp.bfloat16


def dot_nt(a, b):
    return lax.dot_general(a, b, (((1,), (1,)), ((), ())), preferred_element_type=F32)


def dot_tn(a, b):
    return lax.dot_general(a, b, (((0,), (0,)), ((), ())), preferred_element_type=F32)


def dot_nn(a, b):
    return jnp.dot(a, b, preferred_element_type=F32)


def split_two(x):
    high = x.astype(BF16)
    return high, (x - high.astype(F32)).astype(BF16)


def body(
    n_dp,
    n_ctx,
    group,
    q_ref,
    k_ref,
    v_ref,
    og_ref,
    seg_row_ref,
    seg_col_ref,
    f_ref,
    p_ref,
    m1_ref,
    m2_ref,
    bias_ref,
    qg_ref,
    up_ref,
    m1_out,
    m2_out,
    qs,
    gs,
    kall,
    vall,
    seg_all,
    kvacc,
    kv_in,
    kv_pair,
    pall,
    fcat,
    gacc,
    pp,
    cx,
    sb,
    rb,
    dall,
    dother,
    dfull,
    kvs_send,
    kvs_recv,
    rs_send,
    rs_recv,
    p_send,
    p_recv,
    one_send,
    one_recv,
    local_sem,
    red_send,
    red_recv,
    dir_send,
    dir_recv,
):
    tok = q_ref.shape[0]
    hd = k_ref.shape[1]
    seq = n_ctx * tok
    scale = 1.0 / math.sqrt(hd)
    d = lax.axis_index("dp")
    c = lax.axis_index("ctx")
    core = lax.rem(c, 2)
    other = c + 1 - 2 * core
    half_ctx = n_ctx // 2
    chips = n_dp * half_ctx
    chip = d * half_ctx + c // 2
    side = lax.rem(d, 2)
    line = d // 2
    lines = n_dp // 2
    mate = d + 1 - 2 * side
    slab = p_ref.shape[0]
    half = slab // 2
    rows = m1_ref.shape[0]

    barrier = pltpu.get_barrier_semaphore()

    def chip_device(index):
        return (index // half_ctx, lax.rem(index, half_ctx) * 2 + core)

    @pl.loop(1, chips)
    def _(step):
        pl.semaphore_signal(
            barrier, inc=1, device_id=chip_device(lax.rem(chip + step, chips)), device_id_type=MESH
        )

    @pl.loop(0, half_ctx)
    def _(step):
        pl.semaphore_signal(
            barrier, inc=1, device_id=(d, step * 2 + 1 - core), device_id_type=MESH
        )

    def remote(src, dst, send, recv, device):
        return pltpu.make_async_remote_copy(
            src_ref=src, dst_ref=dst, send_sem=send, recv_sem=recv, device_id=device, device_id_type=MESH
        )

    def own_feature_copy(index):
        return pltpu.make_async_copy(
            f_ref.at[:, pl.ds(pl.multiple_of(index * slab + core * half, half), half)],
            fcat.at[0, :, pl.ds(index * half, half)],
            local_sem,
        )

    for index in range(n_dp):
        own_feature_copy(index).start()
    pall[d] = p_ref[pl.ds(pl.multiple_of(core * half, half), half), :]
    kall[c] = k_ref[...]
    vall[c] = v_ref[...]
    seg_all[c] = seg_row_ref[...]
    for head in range(HEADS):
        qs[head * tok : (head + 1) * tok, :] = q_ref[:, head * hd : (head + 1) * hd]
        gs[head * tok : (head + 1) * tok, :] = og_ref[:, head * hd : (head + 1) * hd]
    pl.semaphore_wait(barrier, chips - 1 + half_ctx)

    def kvs_copies(step):
        to = lax.rem(c + step, n_ctx)
        return [
            remote(buf.at[c], buf.at[c], kvs_send.at[i, step], kvs_recv.at[i, c], (d, to))
            for i, buf in enumerate((seg_all, kall, vall))
        ]

    for step in range(1, n_ctx):
        for copy in kvs_copies(step):
            copy.start()

    def p_copy(index, way, device_dp):
        return remote(
            pall.at[index], pall.at[index], p_send.at[way, index], p_recv.at[index], (device_dp, c)
        )

    p_copy(d, 2, mate).start()

    @pl.when(line + 1 < lines)
    def _():
        p_copy(d, 0, d + 2).start()

    @pl.when(line > 0)
    def _():
        p_copy(d, 1, d - 2).start()

    def feature_copy(index):
        return remote(
            f_ref.at[:, pl.ds(pl.multiple_of(index * slab + (1 - core) * half, half), half)],
            fcat.at[1, :, pl.ds(index * half, half)],
            one_send.at[0],
            one_recv.at[0],
            (d, other),
        )

    for index in range(n_dp):
        feature_copy(index).start()

    def p_arrived(index):
        p_copy(index, 2, mate).wait_recv()

    def project(index):
        piece = pall[index]
        cols = pl.ds(pl.multiple_of(index * half, half), half)
        gacc[0] += dot_nn(fcat[0, :, cols], piece)
        gacc[1] += dot_nn(fcat[1, :, cols], piece)

    def forward(distance):
        src = line - distance

        @pl.when(src >= 0)
        def _():
            index = src * 2 + side
            p_arrived(index)

            @pl.when(line + 1 < lines)
            def _():
                p_copy(index, 0, d + 2).start()

            p_copy(index, 2, mate).start()

        back = line + distance

        @pl.when(back < lines)
        def _():
            index = back * 2 + side
            p_arrived(index)

            @pl.when(line > 0)
            def _():
                p_copy(index, 1, d - 2).start()

            p_copy(index, 2, mate).start()

    def project_line(distance):
        @pl.when(line - distance >= 0)
        def _():
            project((line - distance) * 2 + side)

        @pl.when(line + distance < lines)
        def _():
            project((line + distance) * 2 + side)

    def project_across(distance):
        @pl.when(line - distance >= 0)
        def _():
            index = (line - distance) * 2 + 1 - side
            p_arrived(index)
            project(index)

        if distance > 0:

            @pl.when(line + distance < lines)
            def _():
                index = (line + distance) * 2 + 1 - side
                p_arrived(index)
                project(index)

    for step in range(1, n_ctx):
        source = lax.rem(c + n_ctx - step, n_ctx)
        for i, buf in enumerate((seg_all, kall, vall)):
            remote(
                buf.at[source], buf.at[source], kvs_send.at[i, step], kvs_recv.at[i, source], (d, other)
            ).wait_recv()

    width = group * tok
    starts = jnp.zeros((8, width), F32)
    ones = jnp.ones((8, tok), BF16)
    for block in range(n_ctx):
        below = jnp.where(seg_all[block] < seg_col_ref[...], 1.0, 0.0).astype(BF16)
        starts = starts + dot_nt(ones, below)
    first_key = starts[0:1, :].astype(jnp.int32)
    lane = lax.broadcasted_iota(jnp.int32, (1, width), 1)
    query_pos = c * tok + lax.rem(lane, tok)
    key_pos = lax.broadcasted_iota(jnp.int32, (seq, width), 0)

    def attend(index):
        at = index * group * tok
        keys = kall[...].reshape(seq, hd)
        vals = vall[...].reshape(seq, hd)
        q_now = qs[at : at + width, :]
        g_now = gs[at : at + width, :]
        allowed = (key_pos <= query_pos) & (key_pos >= first_key)
        scores = jnp.where(allowed, dot_nt(keys, q_now) * scale, -1e30)
        top = jnp.max(scores, axis=0, keepdims=True)
        expo = jnp.exp(scores - top)
        inverse = 1.0 / jnp.sum(expo, axis=0, keepdims=True)
        dprob = dot_nt(vals, g_now)
        probs = expo * inverse
        delta = jnp.sum(probs * dprob, axis=0, keepdims=True)
        dscore = (probs * (dprob - delta)).astype(BF16)
        probs_low = probs.astype(BF16)
        dk = (dot_nn(dscore, q_now) * scale).reshape(n_ctx, tok, hd)
        dv = dot_nn(probs_low, g_now).reshape(n_ctx, tok, hd)
        if index == 0:
            kvacc[:, :, 0:hd] = dk
            kvacc[:, :, hd : 2 * hd] = dv
        else:
            kvacc[:, :, 0:hd] += dk
            kvacc[:, :, hd : 2 * hd] += dv
        dq = (dot_tn(dscore, keys) * scale).astype(BF16)
        for h in range(group):
            head = index * group + h
            qg_ref[:, head * hd : (head + 1) * hd] = dq[h * tok : (h + 1) * tok, :]

    groups = HEADS // group
    for index in range(groups):
        attend(index)
        if index == 0 and lines > 1:
            forward(1)

    def kv_copy(step):
        to = lax.rem(c + step, n_ctx)
        return remote(kvacc.at[to], kv_in.at[c], rs_send.at[step], rs_recv.at[c], (d, to))

    for step in range(1, n_ctx):
        kv_copy(step).start()

    pltpu.make_async_copy(fcat.at[0], fcat.at[0], local_sem).wait()
    remote(fcat.at[1], fcat.at[1], one_send.at[0], one_recv.at[0], (d, other)).wait_recv()
    gacc[...] = jnp.zeros_like(gacc)
    project(d)
    project_across(0)
    if lines > 1:
        project_line(1)
    if lines > 2:
        forward(2)

    total = kvacc[c]
    for step in range(1, n_ctx):
        source = lax.rem(c + n_ctx - step, n_ctx)
        remote(
            kv_in.at[source], kv_in.at[source], rs_send.at[step], rs_recv.at[source], (d, other)
        ).wait_recv()
        total = total + kv_in[source]
    kv_pair[0] = total.astype(BF16)
    kv_copy_pair = remote(
        kv_pair.at[0], kv_pair.at[1], one_send.at[1], one_recv.at[1], (d, other)
    )
    kv_copy_pair.start()

    for distance in range(1, lines):
        if distance > 2:
            forward(distance)
        if distance > 1:
            project_line(distance)
        project_across(distance)
    kv_copy_pair.wait()

    term = jnp.zeros((gacc.shape[2], 2 * hd), F32)
    for part in range(2):
        high, low = split_two(gacc[part])
        kv_now = kv_pair[part]
        term = term + dot_tn(high, kv_now) + dot_tn(low, kv_now)
    for index in range(chips):
        for k in range(2):
            at = (index * 2 + k) * rows
            pp[k, index] = term[at : at + rows, :]
    swap = remote(pp.at[1 - core], cx, one_send.at[2], one_recv.at[2], (d, other))
    swap.start()
    swap.wait()
    sb[...] = pp[core] + cx[...]

    def sum_copy(step):
        to = lax.rem(chip + step, chips)
        return remote(
            sb.at[to], rb.at[chip], red_send.at[step], red_recv.at[chip], chip_device(to)
        )

    @pl.loop(1, chips)
    def _(step):
        sum_copy(step).start()

    rb[chip] = sb[chip]

    @pl.loop(1, chips)
    def _(step):
        source = lax.rem(chip + chips - step, chips)
        remote(
            rb.at[source], rb.at[source], red_send.at[step], red_recv.at[source], chip_device(source)
        ).wait_recv()

    projected = jnp.sum(rb[...], axis=0)
    first_new = BETA_ONE * m1_ref[...] + (1.0 - BETA_ONE) * projected
    second_new = BETA_TWO * m2_ref[...] + (1.0 - BETA_TWO) * projected * projected
    bias_first = bias_ref[0:1, 0:1]
    bias_second = bias_ref[0:1, 1:2]
    m1_out[...] = first_new
    m2_out[...] = second_new
    dall[chip] = first_new / bias_first / (jnp.sqrt(second_new / bias_second) + EPSILON)

    def dir_copy(step):
        to = lax.rem(chip + step, chips)
        return remote(
            dall.at[chip], dall.at[chip], dir_send.at[step], dir_recv.at[chip], chip_device(to)
        )

    @pl.loop(1, chips)
    def _(step):
        dir_copy(step).start()

    @pl.loop(1, chips)
    def _(step):
        source = lax.rem(chip + chips - step, chips)
        remote(
            dall.at[source], dall.at[source], dir_send.at[step], dir_recv.at[source], chip_device(source)
        ).wait_recv()

    swap_dir = remote(dall, dother, one_send.at[3], one_recv.at[3], (d, other))
    swap_dir.start()
    swap_dir.wait()
    even = jnp.where(core == 0, dall[...], dother[...])
    odd = jnp.where(core == 0, dother[...], dall[...])
    for index in range(chips):
        at = index * 2 * rows
        dfull[at : at + rows, :] = even[index]
        dfull[at + rows : at + 2 * rows, :] = odd[index]
    high, low = split_two(dfull[...])
    out_rows = up_ref.shape[0]
    p_rows = p_ref[pl.ds(pl.multiple_of(c * out_rows, out_rows), out_rows), :]
    up_ref[...] = dot_nn(p_rows, high) + dot_nn(p_rows, low)

    for step in range(1, n_ctx):
        for copy in kvs_copies(step):
            copy.wait_send()
        kv_copy(step).wait_send()
    remote(fcat.at[1], fcat.at[1], one_send.at[0], one_recv.at[0], (d, other)).wait_send()

    @pl.loop(1, chips)
    def _(step):
        sum_copy(step).wait_send()
        dir_copy(step).wait_send()

    for distance in range(lines):
        src = line - distance
        back = line + distance

        @pl.when(src >= 0)
        def _():
            p_copy(src * 2 + side, 2, mate).wait_send()

            @pl.when(line + 1 < lines)
            def _():
                p_copy(src * 2 + side, 0, d + 2).wait_send()

        @pl.when(back < lines)
        def _():
            if distance > 0:
                p_copy(back * 2 + side, 2, mate).wait_send()

            @pl.when(line > 0)
            def _():
                p_copy(back * 2 + side, 1, d - 2).wait_send()


def shards(
    n_dp,
    n_ctx,
    queries,
    keys,
    values,
    out_grad,
    segments,
    features,
    projector,
    first_moment,
    second_moment,
    adam_step,
):
    tok, hd = keys.shape[1], keys.shape[2]
    width = features.shape[2]
    slab, rank = projector.shape
    rows, kvw = first_moment.shape
    chips = n_dp * n_ctx // 2
    half = slab // 2
    group = 4 if n_ctx * tok <= 1024 else 1
    step_count = adam_step[0].astype(F32)
    bias = jnp.stack(
        [
            1.0 - jnp.power(F32(BETA_ONE), step_count),
            1.0 - jnp.power(F32(BETA_TWO), step_count),
        ]
    ).reshape(1, 2)
    seg_col = jnp.tile(segments.reshape(tok, 1), (group, 1))
    vmem = pl.BlockSpec(memory_space=pltpu.VMEM)
    hbm = pl.BlockSpec(memory_space=pl.ANY)
    dma = pltpu.SemaphoreType.DMA
    query_grad, update, first_new, second_new = pl.pallas_call(
        functools.partial(body, n_dp, n_ctx, group),
        out_shape=(
            jax.ShapeDtypeStruct((tok, HEADS * hd), BF16),
            jax.ShapeDtypeStruct((width // (n_dp * n_ctx), kvw), F32),
            jax.ShapeDtypeStruct((rows, kvw), F32),
            jax.ShapeDtypeStruct((rows, kvw), F32),
        ),
        in_specs=[vmem] * 6 + [hbm] + [vmem] * 4,
        out_specs=[vmem] * 4,
        scratch_shapes=[
            pltpu.VMEM((HEADS * tok, hd), BF16),
            pltpu.VMEM((HEADS * tok, hd), BF16),
            pltpu.VMEM((n_ctx, tok, hd), BF16),
            pltpu.VMEM((n_ctx, tok, hd), BF16),
            pltpu.VMEM((n_ctx, 1, tok), jnp.int32),
            pltpu.VMEM((n_ctx, tok, kvw), F32),
            pltpu.VMEM((n_ctx, tok, kvw), F32),
            pltpu.VMEM((2, tok, kvw), BF16),
            pltpu.VMEM((n_dp, half, rank), BF16),
            pltpu.VMEM((2, tok, width // 2), BF16),
            pltpu.VMEM((2, tok, rank), F32),
            pltpu.VMEM((2, chips, rows, kvw), F32),
            pltpu.VMEM((chips, rows, kvw), F32),
            pltpu.VMEM((chips, rows, kvw), F32),
            pltpu.VMEM((chips, rows, kvw), F32),
            pltpu.VMEM((chips, rows, kvw), F32),
            pltpu.VMEM((chips, rows, kvw), F32),
            pltpu.VMEM((rank, kvw), F32),
            dma((3, n_ctx)),
            dma((3, n_ctx)),
            dma((n_ctx,)),
            dma((n_ctx,)),
            dma((3, n_dp)),
            dma((n_dp,)),
            dma((4,)),
            dma((4,)),
            dma(()),
            dma((chips,)),
            dma((chips,)),
            dma((chips,)),
            dma((chips,)),
        ],
        compiler_params=pltpu.CompilerParams(
            collective_id=0, has_side_effects=True, vmem_limit_bytes=56 * 2**20
        ),
    )(
        queries[0],
        keys[0],
        values[0],
        out_grad[0],
        segments,
        seg_col,
        features[0],
        projector,
        first_moment,
        second_moment,
        bias,
    )
    return (query_grad[None], update, first_new, second_new)


def solution(mesh):
    in_specs = (
        P("dp", "ctx", None),
        P("dp", "ctx", None),
        P("dp", "ctx", None),
        P("dp", "ctx", None),
        P("dp", "ctx"),
        P("dp", "ctx", None),
        P("dp", None),
        P(("dp", "ctx"), None),
        P(("dp", "ctx"), None),
        P(),
    )
    out_specs = (
        P("dp", "ctx", None),
        P(("dp", "ctx"), None),
        P(("dp", "ctx"), None),
        P(("dp", "ctx"), None),
    )
    fn = functools.partial(shards, mesh.shape["dp"], mesh.shape["ctx"])
    return jax.shard_map(fn, mesh=mesh, in_specs=in_specs, out_specs=out_specs, check_vma=False)
```

```python
import functools
import math

import jax
import jax.numpy as jnp
from jax import lax
from jax.experimental import pallas as pl
from jax.experimental.pallas import tpu as pltpu
from jax.sharding import PartitionSpec as P

HEADS = 8
BETA_ONE = 0.9
BETA_TWO = 0.999
EPSILON = 1e-08
MESH = pl.DeviceIdType.MESH
F32 = jnp.float32
BF16 = jnp.bfloat16


def dot_nt(a, b):
    return lax.dot_general(a, b, (((1,), (1,)), ((), ())), preferred_element_type=F32)


def dot_tn(a, b):
    return lax.dot_general(a, b, (((0,), (0,)), ((), ())), preferred_element_type=F32)


def dot_nn(a, b):
    return jnp.dot(a, b, preferred_element_type=F32)


def split_two(x):
    high = x.astype(BF16)
    return high, (x - high.astype(F32)).astype(BF16)


def body(
    n_dp,
    n_ctx,
    group,
    members,
    wide_four,
    q_ref,
    k_ref,
    v_ref,
    og_ref,
    seg_row_ref,
    f_ref,
    p_ref,
    m1_ref,
    m2_ref,
    step_ref,
    qg_ref,
    up_ref,
    m1_out,
    m2_out,
    qs,
    gs,
    kall,
    vall,
    seg_all,
    kvacc,
    kv_in,
    kv_all,
    pall,
    f2,
    f4,
    gacc,
    pp,
    cx,
    sb,
    rb,
    dual,
    dfull,
    kvs_send,
    kvs_recv,
    rs_send,
    rs_recv,
    p_send,
    p_recv,
    one_send,
    one_recv,
    local_sem,
    red_send,
    red_recv,
    dir_send,
    dir_recv,
    fwd_send,
    fwd_recv,
    mem_send,
    mem_recv,
):
    tok = q_ref.shape[0]
    hd = k_ref.shape[1]
    seq = n_ctx * tok
    scale = 1.0 / math.sqrt(hd)
    d = lax.axis_index("dp")
    c = lax.axis_index("ctx")
    core = lax.rem(c, 2)
    other = c + 1 - 2 * core
    half_ctx = n_ctx // 2
    chips = n_dp * half_ctx
    chip = d * half_ctx + c // 2
    side = lax.rem(d, 2)
    line = d // 2
    lines = n_dp // 2
    mate = d + 1 - 2 * side
    slab = p_ref.shape[0]
    wide_two = (slab - members * wide_four) // 2
    rows = m1_ref.shape[0]
    spot = lax.rem(c, members)
    base = c - spot
    near = spot + 1 - 2 * core

    barrier = pltpu.get_barrier_semaphore()

    def chip_device(index):
        return (index // half_ctx, lax.rem(index, half_ctx) * 2 + core)

    @pl.loop(1, chips)
    def _(step):
        pl.semaphore_signal(
            barrier, inc=1, device_id=chip_device(lax.rem(chip + step, chips)), device_id_type=MESH
        )

    @pl.loop(0, half_ctx)
    def _(step):
        pl.semaphore_signal(
            barrier, inc=1, device_id=(d, step * 2 + 1 - core), device_id_type=MESH
        )

    def remote(src, dst, send, recv, device):
        return pltpu.make_async_remote_copy(
            src_ref=src, dst_ref=dst, send_sem=send, recv_sem=recv, device_id=device, device_id_type=MESH
        )

    def two_at(index, of_core):
        start = index * slab + members * wide_four + of_core * wide_two
        return pl.ds(pl.multiple_of(start, 128), wide_two)

    def four_at(index, of_spot):
        return pl.ds(pl.multiple_of(index * slab + of_spot * wide_four, 128), wide_four)

    def two_to(index):
        return pl.ds(index * wide_two, wide_two)

    def four_to(index):
        return pl.ds(index * wide_four, wide_four)

    for index in range(n_dp):
        pltpu.make_async_copy(
            f_ref.at[:, two_at(index, core)], f2.at[0, :, two_to(index)], local_sem.at[0]
        ).start()
        if wide_four:
            pltpu.make_async_copy(
                f_ref.at[:, four_at(index, spot)], f4.at[spot, :, four_to(index)], local_sem.at[1]
            ).start()
    if wide_four:
        pall[d, 0:wide_four, :] = p_ref[four_at(0, spot), :]
    pall[d, wide_four : wide_four + wide_two, :] = p_ref[two_at(0, core), :]
    kall[c] = k_ref[...]
    vall[c] = v_ref[...]
    seg_all[c] = seg_row_ref[...]
    for head in range(HEADS):
        qs[head * tok : (head + 1) * tok, :] = q_ref[:, head * hd : (head + 1) * hd]
        gs[head * tok : (head + 1) * tok, :] = og_ref[:, head * hd : (head + 1) * hd]
    pl.semaphore_wait(barrier, chips - 1 + half_ctx)

    def kvs_copies(step):
        to = lax.rem(c + step, n_ctx)
        return [
            remote(buf.at[c], buf.at[c], kvs_send.at[i, step], kvs_recv.at[i, c], (d, to))
            for i, buf in enumerate((seg_all, kall, vall))
        ]

    for step in range(1, n_ctx):
        for copy in kvs_copies(step):
            copy.start()

    def p_copy(index, way, device_dp):
        return remote(
            pall.at[index], pall.at[index], p_send.at[way, index], p_recv.at[index], (device_dp, c)
        )

    p_copy(d, 2, mate).start()

    @pl.when(line + 1 < lines)
    def _():
        p_copy(d, 0, d + 2).start()

    @pl.when(line > 0)
    def _():
        p_copy(d, 1, d - 2).start()

    def member(step):
        return lax.rem(spot + step, members)

    def four_copy(step, index):
        return remote(
            f_ref.at[:, four_at(index, member(step))],
            f4.at[spot, :, four_to(index)],
            mem_send.at[0, step],
            mem_recv.at[0, spot],
            (d, base + member(step)),
        )

    if wide_four:
        for index in range(n_dp):
            for step in range(1, members):
                four_copy(step, index).start()
    for index in range(n_dp):
        remote(
            f_ref.at[:, two_at(index, 1 - core)],
            f2.at[1, :, two_to(index)],
            one_send.at[0],
            one_recv.at[0],
            (d, other),
        ).start()

    def p_arrived(index):
        p_copy(index, 2, mate).wait_recv()

    def project(index):
        cols = pl.ds(pl.multiple_of(index * wide_two, 128), wide_two)
        piece = pall[index, wide_four : wide_four + wide_two, :]
        gacc[spot] += dot_nn(f2[0, :, cols], piece)
        gacc[near] += dot_nn(f2[1, :, cols], piece)
        if wide_four:
            cols = pl.ds(pl.multiple_of(index * wide_four, 128), wide_four)
            lhs = f4[:, :, cols].reshape(members * tok, wide_four)
            out = dot_nn(lhs, pall[index, 0:wide_four, :])
            gacc[...] += out.reshape(members, tok, out.shape[1])

    def forward(distance):
        src = line - distance

        @pl.when(src >= 0)
        def _():
            index = src * 2 + side
            p_arrived(index)

            @pl.when(line + 1 < lines)
            def _():
                p_copy(index, 0, d + 2).start()

            p_copy(index, 2, mate).start()

        back = line + distance

        @pl.when(back < lines)
        def _():
            index = back * 2 + side
            p_arrived(index)

            @pl.when(line > 0)
            def _():
                p_copy(index, 1, d - 2).start()

            p_copy(index, 2, mate).start()

    def project_line(distance):
        @pl.when(line - distance >= 0)
        def _():
            project((line - distance) * 2 + side)

        @pl.when(line + distance < lines)
        def _():
            project((line + distance) * 2 + side)

    def project_across(distance):
        @pl.when(line - distance >= 0)
        def _():
            index = (line - distance) * 2 + 1 - side
            p_arrived(index)
            project(index)

        if distance > 0:

            @pl.when(line + distance < lines)
            def _():
                index = (line + distance) * 2 + 1 - side
                p_arrived(index)
                project(index)

    for step in range(1, n_ctx):
        source = lax.rem(c + n_ctx - step, n_ctx)
        for i, buf in enumerate((seg_all, kall, vall)):
            remote(
                buf.at[source], buf.at[source], kvs_send.at[i, step], kvs_recv.at[i, source], (d, other)
            ).wait_recv()

    width = group * tok
    starts = jnp.zeros((8, width), F32)
    ones = jnp.ones((8, tok), BF16)
    turn = lax.broadcasted_iota(jnp.int32, (width, tok), 0) - lax.broadcasted_iota(
        jnp.int32, (width, tok), 1
    )
    same = jnp.where(lax.rem(turn + tok, tok) == 0, 1.0, 0.0).astype(BF16)
    own_row = jnp.broadcast_to(seg_row_ref[...], (8, tok)).astype(F32).astype(BF16)
    own_col = dot_nt(same, own_row)[:, 0:1]
    for block in range(n_ctx):
        below = jnp.where(seg_all[block].astype(F32) < own_col, 1.0, 0.0).astype(BF16)
        starts = starts + dot_nt(ones, below)
    first_key = starts[0:1, :].astype(jnp.int32)
    lane = lax.broadcasted_iota(jnp.int32, (1, width), 1)
    query_pos = c * tok + lax.rem(lane, tok)
    key_pos = lax.broadcasted_iota(jnp.int32, (seq, width), 0)

    def attend(index):
        at = index * group * tok
        keys = kall[...].reshape(seq, hd)
        vals = vall[...].reshape(seq, hd)
        q_now = qs[at : at + width, :]
        g_now = gs[at : at + width, :]
        allowed = (key_pos <= query_pos) & (key_pos >= first_key)
        scores = jnp.where(allowed, dot_nt(keys, q_now) * scale, -1e30)
        top = jnp.max(scores, axis=0, keepdims=True)
        expo = jnp.exp(scores - top)
        inverse = 1.0 / jnp.sum(expo, axis=0, keepdims=True)
        dprob = dot_nt(vals, g_now)
        probs = expo * inverse
        delta = jnp.sum(probs * dprob, axis=0, keepdims=True)
        dscore = (probs * (dprob - delta)).astype(BF16)
        probs_low = probs.astype(BF16)
        dk = (dot_nn(dscore, q_now) * scale).reshape(n_ctx, tok, hd)
        dv = dot_nn(probs_low, g_now).reshape(n_ctx, tok, hd)
        if index == 0:
            kvacc[:, :, 0:hd] = dk
            kvacc[:, :, hd : 2 * hd] = dv
        else:
            kvacc[:, :, 0:hd] += dk
            kvacc[:, :, hd : 2 * hd] += dv
        dq = (dot_tn(dscore, keys) * scale).astype(BF16)
        for h in range(group):
            head = index * group + h
            qg_ref[:, head * hd : (head + 1) * hd] = dq[h * tok : (h + 1) * tok, :]

    groups = HEADS // group
    for index in range(groups):
        attend(index)
        if index == 0 and lines > 1:
            forward(1)

    def kv_copy(step):
        to = lax.rem(c + step, n_ctx)
        return remote(kvacc.at[to], kv_in.at[c], rs_send.at[step], rs_recv.at[c], (d, to))

    for step in range(1, n_ctx):
        kv_copy(step).start()

    pltpu.make_async_copy(f2.at[0], f2.at[0], local_sem.at[0]).wait()
    remote(f2.at[1], f2.at[1], one_send.at[0], one_recv.at[0], (d, other)).wait_recv()
    if wide_four:
        pltpu.make_async_copy(f4.at[spot], f4.at[spot], local_sem.at[1]).wait()
        for step in range(1, members):
            source = lax.rem(spot + members - step, members)
            remote(
                f4.at[source], f4.at[source], mem_send.at[0, step], mem_recv.at[0, source], (d, other)
            ).wait_recv()
    gacc[...] = jnp.zeros_like(gacc)
    project(d)
    project_across(0)
    if lines > 1:
        project_line(1)
    if lines > 2:
        forward(2)

    total = kvacc[c]
    for step in range(1, n_ctx):
        source = lax.rem(c + n_ctx - step, n_ctx)
        remote(
            kv_in.at[source], kv_in.at[source], rs_send.at[step], rs_recv.at[source], (d, other)
        ).wait_recv()
        total = total + kv_in[source]
    kv_all[spot] = total.astype(BF16)

    def kv_low_copy(step):
        return remote(
            kv_all.at[spot],
            kv_all.at[spot],
            mem_send.at[1, step],
            mem_recv.at[1, spot],
            (d, base + member(step)),
        )

    for step in range(1, members):
        kv_low_copy(step).start()

    for distance in range(1, lines):
        if distance > 2:
            forward(distance)
        if distance > 1:
            project_line(distance)
        project_across(distance)
    for step in range(1, members):
        source = lax.rem(spot + members - step, members)
        remote(
            kv_all.at[source], kv_all.at[source], mem_send.at[1, step], mem_recv.at[1, source], (d, other)
        ).wait_recv()

    kv_flat = kv_all[...].reshape(members * tok, 2 * hd)
    high, low = split_two(gacc[...].reshape(members * tok, gacc.shape[2]))
    term = dot_tn(high, kv_flat) + dot_tn(low, kv_flat)
    for index in range(chips):
        for k in range(2):
            at = (index * 2 + k) * rows
            pp[k, index] = term[at : at + rows, :]
    swap = remote(pp.at[1 - core], cx, one_send.at[2], one_recv.at[2], (d, other))
    swap.start()
    swap.wait()
    sb[...] = pp[core] + cx[...]

    def sum_copy(step):
        to = lax.rem(chip + step, chips)
        return remote(
            sb.at[to], rb.at[chip], red_send.at[step], red_recv.at[chip], chip_device(to)
        )

    @pl.loop(1, chips)
    def _(step):
        sum_copy(step).start()

    rb[chip] = sb[chip]

    @pl.loop(1, chips)
    def _(step):
        source = lax.rem(chip + chips - step, chips)
        remote(
            rb.at[source], rb.at[source], red_send.at[step], red_recv.at[source], chip_device(source)
        ).wait_recv()

    projected = jnp.sum(rb[...], axis=0)
    first_new = BETA_ONE * m1_ref[...] + (1.0 - BETA_ONE) * projected
    second_new = BETA_TWO * m2_ref[...] + (1.0 - BETA_TWO) * projected * projected
    count = jnp.full((1, 2 * hd), step_ref[0], jnp.int32)

    def one_less_power(beta):
        power = jnp.ones((1, 2 * hd), F32)
        square = jnp.full((1, 2 * hd), beta, F32)
        for bit in range(31):
            power = jnp.where((count >> bit) & 1 == 1, power * square, power)
            square = square * square
        return 1.0 - power

    bias_first = one_less_power(BETA_ONE)
    bias_second = one_less_power(BETA_TWO)
    m1_out[...] = first_new
    m2_out[...] = second_new
    direction = first_new / bias_first / (jnp.sqrt(second_new / bias_second) + EPSILON)
    dual[core, chip] = direction.astype(dual.dtype)

    def dir_copy(step):
        to = lax.rem(chip + step, chips)
        return remote(
            dual.at[core, chip],
            dual.at[core, chip],
            dir_send.at[step],
            dir_recv.at[chip],
            chip_device(to),
        )

    def dir_pass(index):
        return remote(
            dual.at[core, index],
            dual.at[core, index],
            fwd_send.at[index],
            fwd_recv.at[index],
            (d, other),
        )

    @pl.loop(1, chips)
    def _(step):
        dir_copy(step).start()

    dir_pass(chip).start()

    @pl.loop(1, chips)
    def _(step):
        source = lax.rem(chip + chips - step, chips)
        remote(
            dual.at[core, source],
            dual.at[core, source],
            dir_send.at[step],
            dir_recv.at[source],
            chip_device(source),
        ).wait_recv()
        dir_pass(source).start()

    @pl.loop(0, chips)
    def _(index):
        remote(
            dual.at[1 - core, index],
            dual.at[1 - core, index],
            fwd_send.at[index],
            fwd_recv.at[index],
            (d, other),
        ).wait_recv()

    for index in range(chips):
        at = index * 2 * rows
        dfull[at : at + rows, :] = dual[0, index]
        dfull[at + rows : at + 2 * rows, :] = dual[1, index]
    out_rows = up_ref.shape[0]
    p_rows = p_ref[pl.ds(pl.multiple_of(c * out_rows, out_rows), out_rows), :]
    if dfull.dtype == BF16:
        up_ref[...] = dot_nn(p_rows, dfull[...])
    else:
        high, low = split_two(dfull[...])
        up_ref[...] = dot_nn(p_rows, high) + dot_nn(p_rows, low)

    for step in range(1, n_ctx):
        for copy in kvs_copies(step):
            copy.wait_send()
        kv_copy(step).wait_send()
    remote(f2.at[1], f2.at[1], one_send.at[0], one_recv.at[0], (d, other)).wait_send()
    for step in range(1, members):
        kv_low_copy(step).wait_send()
        if wide_four:
            remote(
                f4.at[0], f4.at[0], mem_send.at[0, step], mem_recv.at[0, 0], (d, other)
            ).wait_send()

    @pl.loop(0, chips)
    def _(index):
        dir_pass(index).wait_send()

    @pl.loop(1, chips)
    def _(step):
        sum_copy(step).wait_send()
        dir_copy(step).wait_send()

    for distance in range(lines):
        src = line - distance
        back = line + distance

        @pl.when(src >= 0)
        def _():
            p_copy(src * 2 + side, 2, mate).wait_send()

            @pl.when(line + 1 < lines)
            def _():
                p_copy(src * 2 + side, 0, d + 2).wait_send()

        @pl.when(back < lines)
        def _():
            if distance > 0:
                p_copy(back * 2 + side, 2, mate).wait_send()

            @pl.when(line > 0)
            def _():
                p_copy(back * 2 + side, 1, d - 2).wait_send()


def hand_over(a, b, c, d, a_out, b_out, c_out, d_out, sems):
    pairs = ((a, a_out), (b, b_out), (c, c_out), (d, d_out))
    copies = [pltpu.make_async_copy(x, y, sems.at[i]) for i, (x, y) in enumerate(pairs)]
    for copy in copies:
        copy.start()
    for copy in copies:
        copy.wait()


def shards(
    n_dp,
    n_ctx,
    queries,
    keys,
    values,
    out_grad,
    segments,
    features,
    projector,
    first_moment,
    second_moment,
    adam_step,
):
    tok, hd = keys.shape[1], keys.shape[2]
    width = features.shape[2]
    slab, rank = projector.shape
    rows, kvw = first_moment.shape
    chips = n_dp * n_ctx // 2
    group = 4 if n_ctx * tok <= 1024 else 1
    members, wide_four = (4, slab // 8) if slab % 1024 == 0 and n_ctx % 4 == 0 else (2, 0)
    wide_two = (slab - members * wide_four) // 2
    dir_type = BF16 if rows % 16 == 0 else F32
    vmem = pl.BlockSpec(memory_space=pltpu.VMEM)
    hbm = pl.BlockSpec(memory_space=pl.ANY)
    dma = pltpu.SemaphoreType.DMA
    results = pl.pallas_call(
        functools.partial(body, n_dp, n_ctx, group, members, wide_four),
        out_shape=(
            jax.ShapeDtypeStruct((tok, HEADS * hd), BF16),
            jax.ShapeDtypeStruct((width // (n_dp * n_ctx), kvw), F32),
            jax.ShapeDtypeStruct((rows, kvw), F32),
            jax.ShapeDtypeStruct((rows, kvw), F32),
        ),
        in_specs=[vmem] * 5 + [hbm] + [vmem] * 3 + [pl.BlockSpec(memory_space=pltpu.SMEM)],
        out_specs=[vmem] * 4,
        scratch_shapes=[
            pltpu.VMEM((HEADS * tok, hd), BF16),
            pltpu.VMEM((HEADS * tok, hd), BF16),
            pltpu.VMEM((n_ctx, tok, hd), BF16),
            pltpu.VMEM((n_ctx, tok, hd), BF16),
            pltpu.VMEM((n_ctx, 1, tok), jnp.int32),
            pltpu.VMEM((n_ctx, tok, kvw), F32),
            pltpu.VMEM((n_ctx, tok, kvw), F32),
            pltpu.VMEM((members, tok, kvw), BF16),
            pltpu.VMEM((n_dp, wide_four + wide_two, rank), BF16),
            pltpu.VMEM((2, tok, n_dp * wide_two), BF16),
            pltpu.VMEM((members, tok, n_dp * max(wide_four, 128)), BF16),
            pltpu.VMEM((members, tok, rank), F32),
            pltpu.VMEM((2, chips, rows, kvw), F32),
            pltpu.VMEM((chips, rows, kvw), F32),
            pltpu.VMEM((chips, rows, kvw), F32),
            pltpu.VMEM((chips, rows, kvw), F32),
            pltpu.VMEM((2, chips, rows, kvw), dir_type),
            pltpu.VMEM((rank, kvw), dir_type),
            dma((3, n_ctx)),
            dma((3, n_ctx)),
            dma((n_ctx,)),
            dma((n_ctx,)),
            dma((3, n_dp)),
            dma((n_dp,)),
            dma((4,)),
            dma((4,)),
            dma((2,)),
            dma((chips,)),
            dma((chips,)),
            dma((chips,)),
            dma((chips,)),
            dma((chips,)),
            dma((chips,)),
            dma((2, members)),
            dma((2, members)),
        ],
        compiler_params=pltpu.CompilerParams(
            collective_id=0, has_side_effects=True, vmem_limit_bytes=56 * 2**20
        ),
    )(
        queries[0],
        keys[0],
        values[0],
        out_grad[0],
        segments,
        features[0],
        projector,
        first_moment,
        second_moment,
        adam_step,
    )
    query_grad, update, first_new, second_new = pl.pallas_call(
        hand_over,
        out_shape=tuple(jax.ShapeDtypeStruct(r.shape, r.dtype) for r in results),
        in_specs=[hbm] * 4,
        out_specs=[hbm] * 4,
        scratch_shapes=[dma((4,))],
        compiler_params=pltpu.CompilerParams(vmem_limit_bytes=60 * 2**20),
    )(*results)
    return (query_grad[None], update, first_new, second_new)


def solution(mesh):
    in_specs = (
        P("dp", "ctx", None),
        P("dp", "ctx", None),
        P("dp", "ctx", None),
        P("dp", "ctx", None),
        P("dp", "ctx"),
        P("dp", "ctx", None),
        P("dp", None),
        P(("dp", "ctx"), None),
        P(("dp", "ctx"), None),
        P(),
    )
    out_specs = (
        P("dp", "ctx", None),
        P(("dp", "ctx"), None),
        P(("dp", "ctx"), None),
        P(("dp", "ctx"), None),
    )
    fn = functools.partial(shards, mesh.shape["dp"], mesh.shape["ctx"])
    return jax.shard_map(fn, mesh=mesh, in_specs=in_specs, out_specs=out_specs, check_vma=False)
```

```python
import functools
import math

import jax
import jax.numpy as jnp
from jax import lax
from jax.experimental import pallas as pl
from jax.experimental.pallas import tpu as pltpu
from jax.sharding import PartitionSpec as P

HEADS = 8
BETA_ONE = 0.9
BETA_TWO = 0.999
EPSILON = 1e-08
MESH = pl.DeviceIdType.MESH
F32 = jnp.float32
BF16 = jnp.bfloat16


def dot_nt(a, b):
    return lax.dot_general(a, b, (((1,), (1,)), ((), ())), preferred_element_type=F32)


def dot_tn(a, b):
    return lax.dot_general(a, b, (((0,), (0,)), ((), ())), preferred_element_type=F32)


def dot_nn(a, b):
    return jnp.dot(a, b, preferred_element_type=F32)


def split_two(x):
    high = x.astype(BF16)
    return high, (x - high.astype(F32)).astype(BF16)


def body(
    n_dp,
    n_ctx,
    group,
    members,
    wide_four,
    q_ref,
    k_ref,
    v_ref,
    og_ref,
    seg_row_ref,
    f_ref,
    p_ref,
    m1_ref,
    m2_ref,
    step_ref,
    qg_ref,
    up_ref,
    m1_out,
    m2_out,
    qs,
    gs,
    kall,
    vall,
    seg_all,
    kvacc,
    kv_in,
    kv_sum,
    kv_two,
    kv_all,
    pall,
    f2,
    f4,
    gacc,
    pp,
    cx,
    sb,
    rb,
    dual,
    dfull,
    kvs_send,
    kvs_recv,
    rs_send,
    rs_recv,
    p_send,
    p_recv,
    one_send,
    one_recv,
    local_sem,
    red_send,
    red_recv,
    dir_send,
    dir_recv,
    fwd_send,
    fwd_recv,
    mem_send,
    mem_recv,
):
    tok = q_ref.shape[0]
    hd = k_ref.shape[1]
    seq = n_ctx * tok
    scale = 1.0 / math.sqrt(hd)
    d = lax.axis_index("dp")
    c = lax.axis_index("ctx")
    core = lax.rem(c, 2)
    other = c + 1 - 2 * core
    half_ctx = n_ctx // 2
    chips = n_dp * half_ctx
    chip = d * half_ctx + c // 2
    side = lax.rem(d, 2)
    line = d // 2
    lines = n_dp // 2
    mate = d + 1 - 2 * side
    slab = p_ref.shape[0]
    wide_two = (slab - members * wide_four) // 2
    rows = m1_ref.shape[0]
    spot = lax.rem(c, members)
    base = c - spot
    near = spot + 1 - 2 * core

    barrier = pltpu.get_barrier_semaphore()

    def chip_device(index):
        return (index // half_ctx, lax.rem(index, half_ctx) * 2 + core)

    @pl.loop(1, chips)
    def _(step):
        pl.semaphore_signal(
            barrier, inc=1, device_id=chip_device(lax.rem(chip + step, chips)), device_id_type=MESH
        )

    @pl.loop(0, half_ctx)
    def _(step):
        pl.semaphore_signal(
            barrier, inc=1, device_id=(d, step * 2 + 1 - core), device_id_type=MESH
        )

    def remote(src, dst, send, recv, device):
        return pltpu.make_async_remote_copy(
            src_ref=src, dst_ref=dst, send_sem=send, recv_sem=recv, device_id=device, device_id_type=MESH
        )

    def two_at(index, of_core):
        start = index * slab + members * wide_four + of_core * wide_two
        return pl.ds(pl.multiple_of(start, 128), wide_two)

    def four_at(index, of_spot):
        return pl.ds(pl.multiple_of(index * slab + of_spot * wide_four, 128), wide_four)

    def two_to(index):
        return pl.ds(index * wide_two, wide_two)

    def four_to(index):
        return pl.ds(index * wide_four, wide_four)

    for index in range(n_dp):
        pltpu.make_async_copy(
            f_ref.at[:, two_at(index, core)], f2.at[0, :, two_to(index)], local_sem.at[0]
        ).start()
        if wide_four:
            pltpu.make_async_copy(
                f_ref.at[:, four_at(index, spot)], f4.at[spot, :, four_to(index)], local_sem.at[1]
            ).start()
    if wide_four:
        pall[d, 0:wide_four, :] = p_ref[four_at(0, spot), :]
    pall[d, wide_four : wide_four + wide_two, :] = p_ref[two_at(0, core), :]
    kall[c] = k_ref[...]
    vall[c] = v_ref[...]
    seg_all[c] = seg_row_ref[...]
    for head in range(HEADS):
        qs[head * tok : (head + 1) * tok, :] = q_ref[:, head * hd : (head + 1) * hd]
        gs[head * tok : (head + 1) * tok, :] = og_ref[:, head * hd : (head + 1) * hd]
    pl.semaphore_wait(barrier, chips - 1 + half_ctx)

    def kvs_copies(step):
        to = lax.rem(c + step, n_ctx)
        return [
            remote(buf.at[c], buf.at[c], kvs_send.at[i, step], kvs_recv.at[i, c], (d, to))
            for i, buf in enumerate((seg_all, kall, vall))
        ]

    for step in range(1, n_ctx):
        for copy in kvs_copies(step):
            copy.start()

    def p_copy(index, way, device_dp):
        return remote(
            pall.at[index], pall.at[index], p_send.at[way, index], p_recv.at[index], (device_dp, c)
        )

    p_copy(d, 2, mate).start()

    @pl.when(line + 1 < lines)
    def _():
        p_copy(d, 0, d + 2).start()

    @pl.when(line > 0)
    def _():
        p_copy(d, 1, d - 2).start()

    def member(step):
        return lax.rem(spot + step, members)

    def four_copy(step, index):
        return remote(
            f_ref.at[:, four_at(index, member(step))],
            f4.at[spot, :, four_to(index)],
            mem_send.at[0, step],
            mem_recv.at[0, spot],
            (d, base + member(step)),
        )

    def p_arrived(index):
        p_copy(index, 2, mate).wait_recv()

    def project(index):
        cols = pl.ds(pl.multiple_of(index * wide_two, 128), wide_two)
        piece = pall[index, wide_four : wide_four + wide_two, :]
        gacc[spot] += dot_nn(f2[0, :, cols], piece)
        gacc[near] += dot_nn(f2[1, :, cols], piece)
        if wide_four:
            cols = pl.ds(pl.multiple_of(index * wide_four, 128), wide_four)
            lhs = f4[:, :, cols].reshape(members * tok, wide_four)
            out = dot_nn(lhs, pall[index, 0:wide_four, :])
            gacc[...] += out.reshape(members, tok, out.shape[1])

    def forward(distance):
        src = line - distance

        @pl.when(src >= 0)
        def _():
            index = src * 2 + side
            p_arrived(index)

            @pl.when(line + 1 < lines)
            def _():
                p_copy(index, 0, d + 2).start()

            p_copy(index, 2, mate).start()

        back = line + distance

        @pl.when(back < lines)
        def _():
            index = back * 2 + side
            p_arrived(index)

            @pl.when(line > 0)
            def _():
                p_copy(index, 1, d - 2).start()

            p_copy(index, 2, mate).start()

    def project_line(distance):
        @pl.when(line - distance >= 0)
        def _():
            project((line - distance) * 2 + side)

        @pl.when(line + distance < lines)
        def _():
            project((line + distance) * 2 + side)

    def project_across(distance):
        @pl.when(line - distance >= 0)
        def _():
            index = (line - distance) * 2 + 1 - side
            p_arrived(index)
            project(index)

        if distance > 0:

            @pl.when(line + distance < lines)
            def _():
                index = (line + distance) * 2 + 1 - side
                p_arrived(index)
                project(index)

    for step in range(1, n_ctx):
        source = lax.rem(c + n_ctx - step, n_ctx)
        for i, buf in enumerate((seg_all, kall, vall)):
            remote(
                buf.at[source], buf.at[source], kvs_send.at[i, step], kvs_recv.at[i, source], (d, other)
            ).wait_recv()

    if wide_four:
        for index in range(n_dp):
            for step in range(1, members):
                four_copy(step, index).start()
    for index in range(n_dp):
        remote(
            f_ref.at[:, two_at(index, 1 - core)],
            f2.at[1, :, two_to(index)],
            one_send.at[0],
            one_recv.at[0],
            (d, other),
        ).start()

    width = group * tok
    starts = jnp.zeros((8, width), F32)
    ones = jnp.ones((8, tok), BF16)
    turn = lax.broadcasted_iota(jnp.int32, (width, tok), 0) - lax.broadcasted_iota(
        jnp.int32, (width, tok), 1
    )
    same = jnp.where(lax.rem(turn + tok, tok) == 0, 1.0, 0.0).astype(BF16)
    own_row = jnp.broadcast_to(seg_row_ref[...], (8, tok)).astype(F32).astype(BF16)
    own_col = dot_nt(same, own_row)[:, 0:1]
    for block in range(n_ctx):
        below = jnp.where(seg_all[block].astype(F32) < own_col, 1.0, 0.0).astype(BF16)
        starts = starts + dot_nt(ones, below)
    first_key = starts[0:1, :].astype(jnp.int32)
    lane = lax.broadcasted_iota(jnp.int32, (1, width), 1)
    query_pos = c * tok + lax.rem(lane, tok)
    key_pos = lax.broadcasted_iota(jnp.int32, (seq, width), 0)

    def attend(index):
        at = index * group * tok
        keys = kall[...].reshape(seq, hd)
        vals = vall[...].reshape(seq, hd)
        q_now = qs[at : at + width, :]
        g_now = gs[at : at + width, :]
        allowed = (key_pos <= query_pos) & (key_pos >= first_key)
        scores = jnp.where(allowed, dot_nt(keys, q_now) * scale, -1e30)
        top = jnp.max(scores, axis=0, keepdims=True)
        expo = jnp.exp(scores - top)
        inverse = 1.0 / jnp.sum(expo, axis=0, keepdims=True)
        dprob = dot_nt(vals, g_now)
        probs = expo * inverse
        delta = jnp.sum(probs * dprob, axis=0, keepdims=True)
        dscore = (probs * (dprob - delta)).astype(BF16)
        probs_low = probs.astype(BF16)
        dk = (dot_nn(dscore, q_now) * scale).reshape(n_ctx, tok, hd)
        dv = dot_nn(probs_low, g_now).reshape(n_ctx, tok, hd)
        if index == 0:
            kvacc[:, :, 0:hd] = dk
            kvacc[:, :, hd : 2 * hd] = dv
        else:
            kvacc[:, :, 0:hd] += dk
            kvacc[:, :, hd : 2 * hd] += dv
        dq = (dot_tn(dscore, keys) * scale).astype(BF16)
        for h in range(group):
            head = index * group + h
            qg_ref[:, head * hd : (head + 1) * hd] = dq[h * tok : (h + 1) * tok, :]

    groups = HEADS // group
    for index in range(groups):
        attend(index)
        if index == 0 and lines > 1:
            forward(1)
        if index == groups - 2 and lines > 2:
            forward(2)

    def core_copy(index):
        return remote(
            kvacc.at[index * 2 + 1 - core], kv_in.at[index], rs_send.at[0, index], rs_recv.at[0, index], (d, other)
        )

    place = c // 2

    def kv_copy(step):
        to = lax.rem(place + step, half_ctx)
        return remote(
            kv_sum.at[to], kv_two.at[place], rs_send.at[1, step], rs_recv.at[1, place], (d, to * 2 + core)
        )

    for index in range(half_ctx):
        core_copy(index).start()
    pltpu.make_async_copy(f2.at[0], f2.at[0], local_sem.at[0]).wait()
    remote(f2.at[1], f2.at[1], one_send.at[0], one_recv.at[0], (d, other)).wait_recv()
    if wide_four:
        pltpu.make_async_copy(f4.at[spot], f4.at[spot], local_sem.at[1]).wait()
        for step in range(1, members):
            source = lax.rem(spot + members - step, members)
            remote(
                f4.at[source], f4.at[source], mem_send.at[0, step], mem_recv.at[0, source], (d, other)
            ).wait_recv()
    gacc[...] = jnp.zeros_like(gacc)
    for index in range(half_ctx):
        core_copy(index).wait_recv()
        kv_sum[index] = kvacc[index * 2 + core] + kv_in[index]
    for step in range(1, half_ctx):
        kv_copy(step).start()
    project(d)
    project_across(0)
    if lines > 1:
        project_line(1)
    if lines > 3:
        forward(3)

    total = kv_sum[place]
    for step in range(1, half_ctx):
        source = lax.rem(place + half_ctx - step, half_ctx)
        remote(
            kv_two.at[source], kv_two.at[source], rs_send.at[1, step], rs_recv.at[1, source], (d, other)
        ).wait_recv()
        total = total + kv_two[source]
    kv_all[spot] = total.astype(BF16)

    def kv_low_copy(step):
        return remote(
            kv_all.at[spot],
            kv_all.at[spot],
            mem_send.at[1, step],
            mem_recv.at[1, spot],
            (d, base + member(step)),
        )

    for step in range(1, members):
        kv_low_copy(step).start()

    for distance in range(1, lines):
        if distance > 3:
            forward(distance)
        if distance > 1:
            project_line(distance)
        project_across(distance)
    for step in range(1, members):
        source = lax.rem(spot + members - step, members)
        remote(
            kv_all.at[source], kv_all.at[source], mem_send.at[1, step], mem_recv.at[1, source], (d, other)
        ).wait_recv()

    kv_flat = kv_all[...].reshape(members * tok, 2 * hd)
    high, low = split_two(gacc[...].reshape(members * tok, gacc.shape[2]))
    term = dot_tn(high, kv_flat) + dot_tn(low, kv_flat)
    for index in range(chips):
        for k in range(2):
            at = (index * 2 + k) * rows
            pp[k, index] = term[at : at + rows, :]
    swap = remote(pp.at[1 - core], cx, one_send.at[2], one_recv.at[2], (d, other))
    swap.start()
    swap.wait()
    sb[...] = pp[core] + cx[...]

    def sum_copy(step):
        to = lax.rem(chip + step, chips)
        return remote(
            sb.at[to], rb.at[chip], red_send.at[step], red_recv.at[chip], chip_device(to)
        )

    @pl.loop(1, chips)
    def _(step):
        sum_copy(step).start()

    rb[chip] = sb[chip]

    @pl.loop(1, chips)
    def _(step):
        source = lax.rem(chip + chips - step, chips)
        remote(
            rb.at[source], rb.at[source], red_send.at[step], red_recv.at[source], chip_device(source)
        ).wait_recv()

    projected = jnp.sum(rb[...], axis=0)
    first_new = BETA_ONE * m1_ref[...] + (1.0 - BETA_ONE) * projected
    second_new = BETA_TWO * m2_ref[...] + (1.0 - BETA_TWO) * projected * projected
    count = jnp.full((1, 2 * hd), step_ref[0], jnp.int32)

    def one_less_power(beta):
        power = jnp.ones((1, 2 * hd), F32)
        square = jnp.full((1, 2 * hd), beta, F32)
        for bit in range(31):
            power = jnp.where((count >> bit) & 1 == 1, power * square, power)
            square = square * square
        return 1.0 - power

    bias_first = one_less_power(BETA_ONE)
    bias_second = one_less_power(BETA_TWO)
    m1_out[...] = first_new
    m2_out[...] = second_new
    direction = first_new / bias_first / (jnp.sqrt(second_new / bias_second) + EPSILON)
    dual[core, chip] = direction.astype(dual.dtype)

    def dir_copy(step):
        to = lax.rem(chip + step, chips)
        return remote(
            dual.at[core, chip],
            dual.at[core, chip],
            dir_send.at[step],
            dir_recv.at[chip],
            chip_device(to),
        )

    def dir_pass(index):
        return remote(
            dual.at[core, index],
            dual.at[core, index],
            fwd_send.at[index],
            fwd_recv.at[index],
            (d, other),
        )

    @pl.loop(1, chips)
    def _(step):
        dir_copy(step).start()

    dir_pass(chip).start()

    @pl.loop(1, chips)
    def _(step):
        source = lax.rem(chip + chips - step, chips)
        remote(
            dual.at[core, source],
            dual.at[core, source],
            dir_send.at[step],
            dir_recv.at[source],
            chip_device(source),
        ).wait_recv()
        dir_pass(source).start()

    @pl.loop(0, chips)
    def _(index):
        remote(
            dual.at[1 - core, index],
            dual.at[1 - core, index],
            fwd_send.at[index],
            fwd_recv.at[index],
            (d, other),
        ).wait_recv()

    for index in range(chips):
        at = index * 2 * rows
        dfull[at : at + rows, :] = dual[0, index]
        dfull[at + rows : at + 2 * rows, :] = dual[1, index]
    out_rows = up_ref.shape[0]
    p_rows = p_ref[pl.ds(pl.multiple_of(c * out_rows, out_rows), out_rows), :]
    if dfull.dtype == BF16:
        up_ref[...] = dot_nn(p_rows, dfull[...])
    else:
        high, low = split_two(dfull[...])
        up_ref[...] = dot_nn(p_rows, high) + dot_nn(p_rows, low)

    for step in range(1, n_ctx):
        for copy in kvs_copies(step):
            copy.wait_send()
    for step in range(1, half_ctx):
        kv_copy(step).wait_send()
    for index in range(half_ctx):
        core_copy(index).wait_send()
    remote(f2.at[1], f2.at[1], one_send.at[0], one_recv.at[0], (d, other)).wait_send()
    for step in range(1, members):
        kv_low_copy(step).wait_send()
        if wide_four:
            remote(
                f4.at[0], f4.at[0], mem_send.at[0, step], mem_recv.at[0, 0], (d, other)
            ).wait_send()

    @pl.loop(0, chips)
    def _(index):
        dir_pass(index).wait_send()

    @pl.loop(1, chips)
    def _(step):
        sum_copy(step).wait_send()
        dir_copy(step).wait_send()

    for distance in range(lines):
        src = line - distance
        back = line + distance

        @pl.when(src >= 0)
        def _():
            p_copy(src * 2 + side, 2, mate).wait_send()

            @pl.when(line + 1 < lines)
            def _():
                p_copy(src * 2 + side, 0, d + 2).wait_send()

        @pl.when(back < lines)
        def _():
            if distance > 0:
                p_copy(back * 2 + side, 2, mate).wait_send()

            @pl.when(line > 0)
            def _():
                p_copy(back * 2 + side, 1, d - 2).wait_send()


def hand_over(*refs):
    ins, outs, held, sems = refs[0:4], refs[4:8], refs[8:12], refs[12]
    load = [pltpu.make_async_copy(x, y, sems.at[0, i]) for i, (x, y) in enumerate(zip(ins, held))]
    store = [pltpu.make_async_copy(x, y, sems.at[1, i]) for i, (x, y) in enumerate(zip(held, outs))]
    for copy in load:
        copy.start()
    for first, then in zip(load, store):
        first.wait()
        then.start()
    for copy in store:
        copy.wait()


def shards(
    n_dp,
    n_ctx,
    queries,
    keys,
    values,
    out_grad,
    segments,
    features,
    projector,
    first_moment,
    second_moment,
    adam_step,
):
    tok, hd = keys.shape[1], keys.shape[2]
    width = features.shape[2]
    slab, rank = projector.shape
    rows, kvw = first_moment.shape
    chips = n_dp * n_ctx // 2
    group = 2 if n_ctx * tok <= 1024 else 1
    members, wide_four = (4, slab // 8) if slab % 1024 == 0 and n_ctx % 4 == 0 else (2, 0)
    wide_two = (slab - members * wide_four) // 2
    dir_type = BF16 if rows % 16 == 0 else F32
    vmem = pl.BlockSpec(memory_space=pltpu.VMEM)
    hbm = pl.BlockSpec(memory_space=pl.ANY)
    dma = pltpu.SemaphoreType.DMA
    results = pl.pallas_call(
        functools.partial(body, n_dp, n_ctx, group, members, wide_four),
        out_shape=(
            jax.ShapeDtypeStruct((tok, HEADS * hd), BF16),
            jax.ShapeDtypeStruct((width // (n_dp * n_ctx), kvw), F32),
            jax.ShapeDtypeStruct((rows, kvw), F32),
            jax.ShapeDtypeStruct((rows, kvw), F32),
        ),
        in_specs=[vmem] * 5 + [hbm] + [vmem] * 3 + [pl.BlockSpec(memory_space=pltpu.SMEM)],
        out_specs=[vmem] * 4,
        scratch_shapes=[
            pltpu.VMEM((HEADS * tok, hd), BF16),
            pltpu.VMEM((HEADS * tok, hd), BF16),
            pltpu.VMEM((n_ctx, tok, hd), BF16),
            pltpu.VMEM((n_ctx, tok, hd), BF16),
            pltpu.VMEM((n_ctx, 1, tok), jnp.int32),
            pltpu.VMEM((n_ctx, tok, kvw), F32),
            pltpu.VMEM((n_ctx // 2, tok, kvw), F32),
            pltpu.VMEM((n_ctx // 2, tok, kvw), F32),
            pltpu.VMEM((n_ctx // 2, tok, kvw), F32),
            pltpu.VMEM((members, tok, kvw), BF16),
            pltpu.VMEM((n_dp, wide_four + wide_two, rank), BF16),
            pltpu.VMEM((2, tok, n_dp * wide_two), BF16),
            pltpu.VMEM((members, tok, n_dp * max(wide_four, 128)), BF16),
            pltpu.VMEM((members, tok, rank), F32),
            pltpu.VMEM((2, chips, rows, kvw), F32),
            pltpu.VMEM((chips, rows, kvw), F32),
            pltpu.VMEM((chips, rows, kvw), F32),
            pltpu.VMEM((chips, rows, kvw), F32),
            pltpu.VMEM((2, chips, rows, kvw), dir_type),
            pltpu.VMEM((rank, kvw), dir_type),
            dma((3, n_ctx)),
            dma((3, n_ctx)),
            dma((2, n_ctx // 2)),
            dma((2, n_ctx // 2)),
            dma((3, n_dp)),
            dma((n_dp,)),
            dma((4,)),
            dma((4,)),
            dma((2,)),
            dma((chips,)),
            dma((chips,)),
            dma((chips,)),
            dma((chips,)),
            dma((chips,)),
            dma((chips,)),
            dma((2, members)),
            dma((2, members)),
        ],
        compiler_params=pltpu.CompilerParams(
            collective_id=0, has_side_effects=True, vmem_limit_bytes=56 * 2**20
        ),
    )(
        queries[0],
        keys[0],
        values[0],
        out_grad[0],
        segments,
        features[0],
        projector,
        first_moment,
        second_moment,
        adam_step,
    )
    query_grad, update, first_new, second_new = pl.pallas_call(
        hand_over,
        out_shape=tuple(jax.ShapeDtypeStruct(r.shape, r.dtype) for r in results),
        in_specs=[hbm] * 4,
        out_specs=[hbm] * 4,
        scratch_shapes=[pltpu.VMEM(r.shape, r.dtype) for r in results] + [dma((2, 4))],
        compiler_params=pltpu.CompilerParams(vmem_limit_bytes=60 * 2**20),
    )(*results)
    return (query_grad[None], update, first_new, second_new)


def solution(mesh):
    in_specs = (
        P("dp", "ctx", None),
        P("dp", "ctx", None),
        P("dp", "ctx", None),
        P("dp", "ctx", None),
        P("dp", "ctx"),
        P("dp", "ctx", None),
        P("dp", None),
        P(("dp", "ctx"), None),
        P(("dp", "ctx"), None),
        P(),
    )
    out_specs = (
        P("dp", "ctx", None),
        P(("dp", "ctx"), None),
        P(("dp", "ctx"), None),
        P(("dp", "ctx"), None),
    )
    fn = functools.partial(shards, mesh.shape["dp"], mesh.shape["ctx"])
    return jax.shard_map(fn, mesh=mesh, in_specs=in_specs, out_specs=out_specs, check_vma=False)
```

```python
import functools
import math

import jax
import jax.numpy as jnp
from jax import lax
from jax.experimental import pallas as pl
from jax.experimental.pallas import tpu as pltpu
from jax.sharding import PartitionSpec as P

HEADS = 8
BETA_ONE = 0.9
BETA_TWO = 0.999
EPSILON = 1e-08
MESH = pl.DeviceIdType.MESH
F32 = jnp.float32
BF16 = jnp.bfloat16


def dot_nt(a, b):
    return lax.dot_general(a, b, (((1,), (1,)), ((), ())), preferred_element_type=F32)


def dot_tn(a, b):
    return lax.dot_general(a, b, (((0,), (0,)), ((), ())), preferred_element_type=F32)


def dot_nn(a, b):
    return jnp.dot(a, b, preferred_element_type=F32)


def split_two(x):
    high = x.astype(BF16)
    return high, (x - high.astype(F32)).astype(BF16)


def body(
    n_dp,
    n_ctx,
    group,
    members,
    wide_four,
    q_ref,
    k_ref,
    v_ref,
    og_ref,
    seg_row_ref,
    f_ref,
    p_ref,
    m1_ref,
    m2_ref,
    step_ref,
    qg_ref,
    up_ref,
    m1_out,
    m2_out,
    qs,
    gs,
    kall,
    vall,
    seg_all,
    kvacc,
    kv_in,
    kv_sum,
    kv_two,
    kv_all,
    pall,
    f2,
    f4,
    gacc,
    pp,
    cx,
    sb,
    rb,
    dual,
    dfull,
    p_own,
    bias,
    kvs_send,
    kvs_recv,
    rs_send,
    rs_recv,
    p_send,
    p_recv,
    one_send,
    one_recv,
    local_sem,
    red_send,
    red_recv,
    dir_send,
    dir_recv,
    fwd_send,
    fwd_recv,
    mem_send,
    mem_recv,
):
    tok = q_ref.shape[0]
    out_rows = up_ref.shape[0]
    hd = k_ref.shape[1]
    seq = n_ctx * tok
    scale = 1.0 / math.sqrt(hd)
    d = lax.axis_index("dp")
    c = lax.axis_index("ctx")
    core = lax.rem(c, 2)
    other = c + 1 - 2 * core
    half_ctx = n_ctx // 2
    chips = n_dp * half_ctx
    chip = d * half_ctx + c // 2
    side = lax.rem(d, 2)
    line = d // 2
    lines = n_dp // 2
    mate = d + 1 - 2 * side
    slab = p_ref.shape[0]
    wide_two = (slab - members * wide_four) // 2
    rows = m1_ref.shape[0]
    spot = lax.rem(c, members)
    base = c - spot
    near = spot + 1 - 2 * core

    barrier = pltpu.get_barrier_semaphore()

    def chip_device(index):
        return (index // half_ctx, lax.rem(index, half_ctx) * 2 + core)

    @pl.loop(1, chips)
    def _(step):
        pl.semaphore_signal(
            barrier, inc=1, device_id=chip_device(lax.rem(chip + step, chips)), device_id_type=MESH
        )

    @pl.loop(0, half_ctx)
    def _(step):
        pl.semaphore_signal(
            barrier, inc=1, device_id=(d, step * 2 + 1 - core), device_id_type=MESH
        )

    def remote(src, dst, send, recv, device):
        return pltpu.make_async_remote_copy(
            src_ref=src, dst_ref=dst, send_sem=send, recv_sem=recv, device_id=device, device_id_type=MESH
        )

    def two_at(index, of_core):
        start = index * slab + members * wide_four + of_core * wide_two
        return pl.ds(pl.multiple_of(start, 128), wide_two)

    def four_at(index, of_spot):
        return pl.ds(pl.multiple_of(index * slab + of_spot * wide_four, 128), wide_four)

    def two_to(index):
        return pl.ds(index * wide_two, wide_two)

    def four_to(index):
        return pl.ds(index * wide_four, wide_four)

    for index in range(n_dp):
        pltpu.make_async_copy(
            f_ref.at[:, two_at(index, core)], f2.at[0, :, two_to(index)], local_sem.at[0]
        ).start()
        if wide_four:
            pltpu.make_async_copy(
                f_ref.at[:, four_at(index, spot)], f4.at[spot, :, four_to(index)], local_sem.at[1]
            ).start()
    if wide_four:
        pltpu.make_async_copy(
            p_ref.at[four_at(0, spot), :], pall.at[d, pl.ds(0, wide_four), :], local_sem.at[6]
        ).start()
    pltpu.make_async_copy(
        p_ref.at[two_at(0, core), :], pall.at[d, pl.ds(wide_four, wide_two), :], local_sem.at[6]
    ).start()
    seg_all[c] = seg_row_ref[...]
    pltpu.make_async_copy(k_ref, kall.at[c], local_sem.at[4]).start()
    pltpu.make_async_copy(v_ref, vall.at[c], local_sem.at[5]).start()
    for head in range(HEADS):
        for i, (wide, packed) in enumerate(((q_ref, qs), (og_ref, gs))):
            pltpu.make_async_copy(
                wide.at[:, pl.ds(head * hd, hd)], packed.at[pl.ds(head * tok, tok), :], local_sem.at[2 + i]
            ).start()
    p_rows_copy = pltpu.make_async_copy(
        p_ref.at[pl.ds(pl.multiple_of(c * out_rows, out_rows), out_rows), :], p_own, local_sem.at[7]
    )
    p_rows_copy.start()
    pl.semaphore_wait(barrier, chips - 1 + half_ctx)

    def kvs_copies(step):
        to = lax.rem(c + step, n_ctx)
        return [
            remote(buf.at[c], buf.at[c], kvs_send.at[i, step], kvs_recv.at[i, c], (d, to))
            for i, buf in enumerate((seg_all, kall, vall))
        ]

    pltpu.make_async_copy(k_ref, kall.at[c], local_sem.at[4]).wait()
    pltpu.make_async_copy(v_ref, vall.at[c], local_sem.at[5]).wait()

    for step in range(1, n_ctx):
        for copy in kvs_copies(step):
            copy.start()

    chunk_rows = (wide_four + wide_two) // 2

    def p_copy(index, way, device_dp, chunk):
        piece = pall.at[index, pl.ds(chunk * chunk_rows, chunk_rows), :]
        return remote(
            piece, piece, p_send.at[way, index, chunk], p_recv.at[index, chunk], (device_dp, c)
        )

    def pass_on(index, chunk, right, left):
        if right:

            @pl.when(line + 1 < lines)
            def _():
                p_copy(index, 0, d + 2, chunk).start()

        if left:

            @pl.when(line > 0)
            def _():
                p_copy(index, 1, d - 2, chunk).start()

        p_copy(index, 2, mate, chunk).start()

    pltpu.make_async_copy(pall.at[d], pall.at[d], local_sem.at[6]).wait()
    for chunk in range(2):
        pass_on(d, chunk, True, True)

    def member(step):
        return lax.rem(spot + step, members)

    def four_copy(step, index):
        return remote(
            f_ref.at[:, four_at(index, member(step))],
            f4.at[spot, :, four_to(index)],
            mem_send.at[0, step],
            mem_recv.at[0, spot],
            (d, base + member(step)),
        )

    def p_arrived(index, chunk):
        p_copy(index, 2, mate, chunk).wait_recv()

    def project(index):
        cols = pl.ds(pl.multiple_of(index * wide_two, 128), wide_two)
        piece = pall[index, wide_four : wide_four + wide_two, :]
        gacc[spot] += dot_nn(f2[0, :, cols], piece)
        gacc[near] += dot_nn(f2[1, :, cols], piece)
        if wide_four:
            cols = pl.ds(pl.multiple_of(index * wide_four, 128), wide_four)
            lhs = f4[:, :, cols].reshape(members * tok, wide_four)
            out = dot_nn(lhs, pall[index, 0:wide_four, :])
            gacc[...] += out.reshape(members, tok, out.shape[1])

    def forward(distance):
        src = line - distance
        back = line + distance
        for chunk in range(2):

            @pl.when(src >= 0)
            def _():
                p_arrived(src * 2 + side, chunk)
                pass_on(src * 2 + side, chunk, True, False)

            @pl.when(back < lines)
            def _():
                p_arrived(back * 2 + side, chunk)
                pass_on(back * 2 + side, chunk, False, True)

    def project_line(distance):
        @pl.when(line - distance >= 0)
        def _():
            project((line - distance) * 2 + side)

        @pl.when(line + distance < lines)
        def _():
            project((line + distance) * 2 + side)

    def project_across(distance):
        @pl.when(line - distance >= 0)
        def _():
            index = (line - distance) * 2 + 1 - side
            p_arrived(index, 0)
            p_arrived(index, 1)
            project(index)

        if distance > 0:

            @pl.when(line + distance < lines)
            def _():
                index = (line + distance) * 2 + 1 - side
                p_arrived(index, 0)
                p_arrived(index, 1)
                project(index)

    for step in range(1, n_ctx):
        source = lax.rem(c + n_ctx - step, n_ctx)
        for i, buf in enumerate((seg_all, kall, vall)):
            remote(
                buf.at[source], buf.at[source], kvs_send.at[i, step], kvs_recv.at[i, source], (d, other)
            ).wait_recv()

    if wide_four:
        for index in range(n_dp):
            for step in range(1, members):
                four_copy(step, index).start()
    for index in range(n_dp):
        remote(
            f_ref.at[:, two_at(index, 1 - core)],
            f2.at[1, :, two_to(index)],
            one_send.at[0],
            one_recv.at[0],
            (d, other),
        ).start()

    width = group * tok
    starts = jnp.zeros((8, width), F32)
    ones = jnp.ones((8, tok), BF16)
    turn = lax.broadcasted_iota(jnp.int32, (width, tok), 0) - lax.broadcasted_iota(
        jnp.int32, (width, tok), 1
    )
    same = jnp.where(lax.rem(turn + tok, tok) == 0, 1.0, 0.0).astype(BF16)
    own_row = jnp.broadcast_to(seg_row_ref[...], (8, tok)).astype(F32).astype(BF16)
    own_col = dot_nt(same, own_row)[:, 0:1]
    for block in range(n_ctx):
        below = jnp.where(seg_all[block].astype(F32) < own_col, 1.0, 0.0).astype(BF16)
        starts = starts + dot_nt(ones, below)
    first_key = starts[0:1, :].astype(jnp.int32)
    lane = lax.broadcasted_iota(jnp.int32, (1, width), 1)
    query_pos = c * tok + lax.rem(lane, tok)
    key_pos = lax.broadcasted_iota(jnp.int32, (seq, width), 0)

    bias[...] = jnp.where((key_pos <= query_pos) & (key_pos >= first_key), 0.0, -1e30)
    pltpu.make_async_copy(qs, qs, local_sem.at[2]).wait()
    pltpu.make_async_copy(gs, gs, local_sem.at[3]).wait()

    def attend(index):
        at = index * group * tok
        keys = kall[...].reshape(seq, hd)
        vals = vall[...].reshape(seq, hd)
        q_now = qs[at : at + width, :]
        g_now = gs[at : at + width, :]
        scores = dot_nt(keys, q_now) * (scale * math.log2(math.e)) + bias[...]
        top = jnp.max(scores, axis=0, keepdims=True)
        expo = jnp.exp2(scores - top)
        inverse = 1.0 / jnp.sum(expo, axis=0, keepdims=True)
        dprob = dot_nt(vals, g_now)
        probs = expo * inverse
        delta = jnp.sum(probs * dprob, axis=0, keepdims=True)
        dscore = (probs * (dprob - delta)).astype(BF16)
        probs_low = probs.astype(BF16)
        dk = (dot_nn(dscore, q_now) * scale).reshape(n_ctx, tok, hd)
        dv = dot_nn(probs_low, g_now).reshape(n_ctx, tok, hd)
        if index == 0:
            kvacc[:, :, 0:hd] = dk
            kvacc[:, :, hd : 2 * hd] = dv
        else:
            kvacc[:, :, 0:hd] += dk
            kvacc[:, :, hd : 2 * hd] += dv
        dq = (dot_tn(dscore, keys) * scale).astype(BF16)
        for h in range(group):
            head = index * group + h
            qg_ref[:, head * hd : (head + 1) * hd] = dq[h * tok : (h + 1) * tok, :]

    groups = HEADS // group
    for index in range(groups):
        attend(index)
        if index == 0 and lines > 1:
            forward(1)
        if index == groups - 2 and lines > 2:
            forward(2)

    def core_copy(index):
        return remote(
            kvacc.at[index * 2 + 1 - core], kv_in.at[index], rs_send.at[0, index], rs_recv.at[0, index], (d, other)
        )

    place = c // 2

    def kv_copy(step):
        to = lax.rem(place + step, half_ctx)
        return remote(
            kv_sum.at[to], kv_two.at[place], rs_send.at[1, step], rs_recv.at[1, place], (d, to * 2 + core)
        )

    for index in range(half_ctx):
        core_copy(index).start()
    pltpu.make_async_copy(f2.at[0], f2.at[0], local_sem.at[0]).wait()
    remote(f2.at[1], f2.at[1], one_send.at[0], one_recv.at[0], (d, other)).wait_recv()
    if wide_four:
        pltpu.make_async_copy(f4.at[spot], f4.at[spot], local_sem.at[1]).wait()
        for step in range(1, members):
            source = lax.rem(spot + members - step, members)
            remote(
                f4.at[source], f4.at[source], mem_send.at[0, step], mem_recv.at[0, source], (d, other)
            ).wait_recv()
    gacc[...] = jnp.zeros_like(gacc)
    for index in range(half_ctx):
        core_copy(index).wait_recv()
        kv_sum[index] = kvacc[index * 2 + core] + kv_in[index]
    for step in range(1, half_ctx):
        kv_copy(step).start()
    project(d)
    project_across(0)
    if lines > 1:
        project_line(1)
    if lines > 3:
        forward(3)

    total = kv_sum[place]
    for step in range(1, half_ctx):
        source = lax.rem(place + half_ctx - step, half_ctx)
        remote(
            kv_two.at[source], kv_two.at[source], rs_send.at[1, step], rs_recv.at[1, source], (d, other)
        ).wait_recv()
        total = total + kv_two[source]
    kv_all[spot] = total.astype(BF16)

    def kv_low_copy(step):
        return remote(
            kv_all.at[spot],
            kv_all.at[spot],
            mem_send.at[1, step],
            mem_recv.at[1, spot],
            (d, base + member(step)),
        )

    for step in range(1, members):
        kv_low_copy(step).start()

    for distance in range(1, lines):
        if distance > 3:
            forward(distance)
        if distance > 1:
            project_line(distance)
        project_across(distance)
    for step in range(1, members):
        source = lax.rem(spot + members - step, members)
        remote(
            kv_all.at[source], kv_all.at[source], mem_send.at[1, step], mem_recv.at[1, source], (d, other)
        ).wait_recv()

    kv_flat = kv_all[...].reshape(members * tok, 2 * hd)
    high, low = split_two(gacc[...].reshape(members * tok, gacc.shape[2]))
    term = dot_tn(high, kv_flat) + dot_tn(low, kv_flat)
    for index in range(chips):
        for k in range(2):
            at = (index * 2 + k) * rows
            pp[k, index] = term[at : at + rows, :]
    swap = remote(pp.at[1 - core], cx, one_send.at[2], one_recv.at[2], (d, other))
    swap.start()
    swap.wait()
    sb[...] = pp[core] + cx[...]

    def sum_copy(step):
        to = lax.rem(chip + step, chips)
        return remote(
            sb.at[to], rb.at[chip], red_send.at[step], red_recv.at[chip], chip_device(to)
        )

    @pl.loop(1, chips)
    def _(step):
        sum_copy(step).start()

    rb[chip] = sb[chip]

    @pl.loop(1, chips)
    def _(step):
        source = lax.rem(chip + chips - step, chips)
        remote(
            rb.at[source], rb.at[source], red_send.at[step], red_recv.at[source], chip_device(source)
        ).wait_recv()

    projected = jnp.sum(rb[...], axis=0)
    first_new = BETA_ONE * m1_ref[...] + (1.0 - BETA_ONE) * projected
    second_new = BETA_TWO * m2_ref[...] + (1.0 - BETA_TWO) * projected * projected
    count = jnp.full((1, 2 * hd), step_ref[0], jnp.int32)

    def one_less_power(beta):
        power = jnp.ones((1, 2 * hd), F32)
        square = jnp.full((1, 2 * hd), beta, F32)
        for bit in range(31):
            power = jnp.where((count >> bit) & 1 == 1, power * square, power)
            square = square * square
        return 1.0 - power

    bias_first = one_less_power(BETA_ONE)
    bias_second = one_less_power(BETA_TWO)
    m1_out[...] = first_new
    m2_out[...] = second_new
    direction = first_new / bias_first / (jnp.sqrt(second_new / bias_second) + EPSILON)
    dual[core, chip] = direction.astype(dual.dtype)

    def dir_copy(step):
        to = lax.rem(chip + step, chips)
        return remote(
            dual.at[core, chip],
            dual.at[core, chip],
            dir_send.at[step],
            dir_recv.at[chip],
            chip_device(to),
        )

    def dir_pass(index):
        return remote(
            dual.at[core, index],
            dual.at[core, index],
            fwd_send.at[index],
            fwd_recv.at[index],
            (d, other),
        )

    @pl.loop(1, chips)
    def _(step):
        dir_copy(step).start()

    dir_pass(chip).start()

    @pl.loop(1, chips)
    def _(step):
        source = lax.rem(chip + chips - step, chips)
        remote(
            dual.at[core, source],
            dual.at[core, source],
            dir_send.at[step],
            dir_recv.at[source],
            chip_device(source),
        ).wait_recv()
        dir_pass(source).start()

    @pl.loop(0, chips)
    def _(index):
        remote(
            dual.at[1 - core, index],
            dual.at[1 - core, index],
            fwd_send.at[index],
            fwd_recv.at[index],
            (d, other),
        ).wait_recv()

    for index in range(chips):
        at = index * 2 * rows
        dfull[at : at + rows, :] = dual[0, index]
        dfull[at + rows : at + 2 * rows, :] = dual[1, index]
    p_rows_copy.wait()
    p_rows = p_own[...]
    if dfull.dtype == BF16:
        up_ref[...] = dot_nn(p_rows, dfull[...])
    else:
        high, low = split_two(dfull[...])
        up_ref[...] = dot_nn(p_rows, high) + dot_nn(p_rows, low)

    for step in range(1, n_ctx):
        for copy in kvs_copies(step):
            copy.wait_send()
    for step in range(1, half_ctx):
        kv_copy(step).wait_send()
    for index in range(half_ctx):
        core_copy(index).wait_send()
    remote(f2.at[1], f2.at[1], one_send.at[0], one_recv.at[0], (d, other)).wait_send()
    for step in range(1, members):
        kv_low_copy(step).wait_send()
        if wide_four:
            remote(
                f4.at[0], f4.at[0], mem_send.at[0, step], mem_recv.at[0, 0], (d, other)
            ).wait_send()

    @pl.loop(0, chips)
    def _(index):
        dir_pass(index).wait_send()

    @pl.loop(1, chips)
    def _(step):
        sum_copy(step).wait_send()
        dir_copy(step).wait_send()

    def sent(index, right, left):
        for chunk in range(2):
            p_copy(index, 2, mate, chunk).wait_send()
            if right:

                @pl.when(line + 1 < lines)
                def _():
                    p_copy(index, 0, d + 2, chunk).wait_send()

            if left:

                @pl.when(line > 0)
                def _():
                    p_copy(index, 1, d - 2, chunk).wait_send()

    sent(d, True, True)
    for distance in range(1, lines):

        @pl.when(line - distance >= 0)
        def _():
            sent((line - distance) * 2 + side, True, False)

        @pl.when(line + distance < lines)
        def _():
            sent((line + distance) * 2 + side, False, True)


def hand_over(*refs):
    ins, outs, held, sems = refs[0:4], refs[4:8], refs[8:12], refs[12]
    load = [pltpu.make_async_copy(x, y, sems.at[0, i]) for i, (x, y) in enumerate(zip(ins, held))]
    store = [pltpu.make_async_copy(x, y, sems.at[1, i]) for i, (x, y) in enumerate(zip(held, outs))]
    for copy in load:
        copy.start()
    for first, then in zip(load, store):
        first.wait()
        then.start()
    for copy in store:
        copy.wait()


def shards(
    n_dp,
    n_ctx,
    queries,
    keys,
    values,
    out_grad,
    segments,
    features,
    projector,
    first_moment,
    second_moment,
    adam_step,
):
    tok, hd = keys.shape[1], keys.shape[2]
    width = features.shape[2]
    slab, rank = projector.shape
    rows, kvw = first_moment.shape
    chips = n_dp * n_ctx // 2
    group = 2 if n_ctx * tok <= 1024 else 1
    members, wide_four = (4, slab // 8) if slab % 1024 == 0 and n_ctx % 4 == 0 else (2, 0)
    wide_two = (slab - members * wide_four) // 2
    dir_type = BF16 if rows % 16 == 0 else F32
    vmem = pl.BlockSpec(memory_space=pltpu.VMEM)
    hbm = pl.BlockSpec(memory_space=pl.ANY)
    dma = pltpu.SemaphoreType.DMA
    results = pl.pallas_call(
        functools.partial(body, n_dp, n_ctx, group, members, wide_four),
        out_shape=(
            jax.ShapeDtypeStruct((tok, HEADS * hd), BF16),
            jax.ShapeDtypeStruct((width // (n_dp * n_ctx), kvw), F32),
            jax.ShapeDtypeStruct((rows, kvw), F32),
            jax.ShapeDtypeStruct((rows, kvw), F32),
        ),
        in_specs=[hbm] * 4 + [vmem] + [hbm] * 2 + [vmem] * 2 + [pl.BlockSpec(memory_space=pltpu.SMEM)],
        out_specs=[vmem] * 4,
        scratch_shapes=[
            pltpu.VMEM((HEADS * tok, hd), BF16),
            pltpu.VMEM((HEADS * tok, hd), BF16),
            pltpu.VMEM((n_ctx, tok, hd), BF16),
            pltpu.VMEM((n_ctx, tok, hd), BF16),
            pltpu.VMEM((n_ctx, 1, tok), jnp.int32),
            pltpu.VMEM((n_ctx, tok, kvw), F32),
            pltpu.VMEM((n_ctx // 2, tok, kvw), F32),
            pltpu.VMEM((n_ctx // 2, tok, kvw), F32),
            pltpu.VMEM((n_ctx // 2, tok, kvw), F32),
            pltpu.VMEM((members, tok, kvw), BF16),
            pltpu.VMEM((n_dp, wide_four + wide_two, rank), BF16),
            pltpu.VMEM((2, tok, n_dp * wide_two), BF16),
            pltpu.VMEM((members, tok, n_dp * max(wide_four, 128)), BF16),
            pltpu.VMEM((members, tok, rank), F32),
            pltpu.VMEM((2, chips, rows, kvw), F32),
            pltpu.VMEM((chips, rows, kvw), F32),
            pltpu.VMEM((chips, rows, kvw), F32),
            pltpu.VMEM((chips, rows, kvw), F32),
            pltpu.VMEM((2, chips, rows, kvw), dir_type),
            pltpu.VMEM((rank, kvw), dir_type),
            pltpu.VMEM((slab // n_ctx, rank), BF16),
            pltpu.VMEM((n_ctx * tok, group * tok), F32),
            dma((3, n_ctx)),
            dma((3, n_ctx)),
            dma((2, n_ctx // 2)),
            dma((2, n_ctx // 2)),
            dma((3, n_dp, 2)),
            dma((n_dp, 2)),
            dma((4,)),
            dma((4,)),
            dma((8,)),
            dma((chips,)),
            dma((chips,)),
            dma((chips,)),
            dma((chips,)),
            dma((chips,)),
            dma((chips,)),
            dma((2, members)),
            dma((2, members)),
        ],
        compiler_params=pltpu.CompilerParams(
            collective_id=0, has_side_effects=True, vmem_limit_bytes=56 * 2**20
        ),
    )(
        queries[0],
        keys[0],
        values[0],
        out_grad[0],
        segments,
        features[0],
        projector,
        first_moment,
        second_moment,
        adam_step,
    )
    query_grad, update, first_new, second_new = pl.pallas_call(
        hand_over,
        out_shape=tuple(jax.ShapeDtypeStruct(r.shape, r.dtype) for r in results),
        in_specs=[hbm] * 4,
        out_specs=[hbm] * 4,
        scratch_shapes=[pltpu.VMEM(r.shape, r.dtype) for r in results] + [dma((2, 4))],
        compiler_params=pltpu.CompilerParams(vmem_limit_bytes=60 * 2**20),
    )(*results)
    return (query_grad[None], update, first_new, second_new)


def solution(mesh):
    in_specs = (
        P("dp", "ctx", None),
        P("dp", "ctx", None),
        P("dp", "ctx", None),
        P("dp", "ctx", None),
        P("dp", "ctx"),
        P("dp", "ctx", None),
        P("dp", None),
        P(("dp", "ctx"), None),
        P(("dp", "ctx"), None),
        P(),
    )
    out_specs = (
        P("dp", "ctx", None),
        P(("dp", "ctx"), None),
        P(("dp", "ctx"), None),
        P(("dp", "ctx"), None),
    )
    fn = functools.partial(shards, mesh.shape["dp"], mesh.shape["ctx"])
    return jax.shard_map(fn, mesh=mesh, in_specs=in_specs, out_specs=out_specs, check_vma=False)
```

```python
import functools
import math

import jax
import jax.numpy as jnp
from jax import lax
from jax.experimental import pallas as pl
from jax.experimental.pallas import tpu as pltpu
from jax.sharding import PartitionSpec as P

HEADS = 8
BETA_ONE = 0.9
BETA_TWO = 0.999
EPSILON = 1e-08
MESH = pl.DeviceIdType.MESH
F32 = jnp.float32
BF16 = jnp.bfloat16


def dot_nt(a, b):
    return lax.dot_general(a, b, (((1,), (1,)), ((), ())), preferred_element_type=F32)


def dot_tn(a, b):
    return lax.dot_general(a, b, (((0,), (0,)), ((), ())), preferred_element_type=F32)


def dot_nn(a, b):
    return jnp.dot(a, b, preferred_element_type=F32)


def split_two(x):
    high = x.astype(BF16)
    return high, (x - high.astype(F32)).astype(BF16)


def body(
    n_dp,
    n_ctx,
    group,
    members,
    wide_four,
    q_ref,
    k_ref,
    v_ref,
    og_ref,
    seg_row_ref,
    f_ref,
    p_ref,
    m1_ref,
    m2_ref,
    step_ref,
    qg_ref,
    up_ref,
    m1_out,
    m2_out,
    qs,
    gs,
    kall,
    vall,
    seg_all,
    kvacc,
    kv_in,
    kv_sum,
    kv_two,
    kv_all,
    pall,
    f2,
    f4,
    gacc,
    pp,
    cx,
    sb,
    rb,
    dual,
    dfull,
    p_own,
    bias,
    kvs_send,
    kvs_recv,
    rs_send,
    rs_recv,
    p_send,
    p_recv,
    one_send,
    one_recv,
    local_sem,
    red_send,
    red_recv,
    dir_send,
    dir_recv,
    fwd_send,
    fwd_recv,
    mem_send,
    mem_recv,
):
    tok = q_ref.shape[0]
    out_rows = up_ref.shape[0]
    hd = k_ref.shape[1]
    seq = n_ctx * tok
    scale = 1.0 / math.sqrt(hd)
    d = lax.axis_index("dp")
    c = lax.axis_index("ctx")
    core = lax.rem(c, 2)
    other = c + 1 - 2 * core
    half_ctx = n_ctx // 2
    chips = n_dp * half_ctx
    chip = d * half_ctx + c // 2
    side = lax.rem(d, 2)
    line = d // 2
    lines = n_dp // 2
    mate = d + 1 - 2 * side
    slab = p_ref.shape[0]
    wide_two = (slab - members * wide_four) // 2
    rows = m1_ref.shape[0]
    spot = lax.rem(c, members)
    base = c - spot
    near = spot + 1 - 2 * core

    barrier = pltpu.get_barrier_semaphore()

    def chip_device(index):
        return (index // half_ctx, lax.rem(index, half_ctx) * 2 + core)

    @pl.loop(1, chips)
    def _(step):
        pl.semaphore_signal(
            barrier, inc=1, device_id=chip_device(lax.rem(chip + step, chips)), device_id_type=MESH
        )

    @pl.loop(0, half_ctx)
    def _(step):
        pl.semaphore_signal(
            barrier, inc=1, device_id=(d, step * 2 + 1 - core), device_id_type=MESH
        )

    def remote(src, dst, send, recv, device):
        return pltpu.make_async_remote_copy(
            src_ref=src, dst_ref=dst, send_sem=send, recv_sem=recv, device_id=device, device_id_type=MESH
        )

    def two_at(index, of_core):
        start = index * slab + members * wide_four + of_core * wide_two
        return pl.ds(pl.multiple_of(start, 128), wide_two)

    def four_at(index, of_spot):
        return pl.ds(pl.multiple_of(index * slab + of_spot * wide_four, 128), wide_four)

    def two_to(index):
        return pl.ds(index * wide_two, wide_two)

    def four_to(index):
        return pl.ds(index * wide_four, wide_four)

    for index in range(n_dp):
        pltpu.make_async_copy(
            f_ref.at[:, two_at(index, core)], f2.at[0, :, two_to(index)], local_sem.at[0]
        ).start()
        if wide_four:
            pltpu.make_async_copy(
                f_ref.at[:, four_at(index, spot)], f4.at[spot, :, four_to(index)], local_sem.at[1]
            ).start()
    if wide_four:
        pltpu.make_async_copy(
            p_ref.at[four_at(0, spot), :], pall.at[d, pl.ds(0, wide_four), :], local_sem.at[6]
        ).start()
    pltpu.make_async_copy(
        p_ref.at[two_at(0, core), :], pall.at[d, pl.ds(wide_four, wide_two), :], local_sem.at[6]
    ).start()
    seg_all[c] = seg_row_ref[...]
    pltpu.make_async_copy(k_ref, kall.at[c], local_sem.at[4]).start()
    pltpu.make_async_copy(v_ref, vall.at[c], local_sem.at[5]).start()
    for head in range(HEADS):
        for i, (wide, packed) in enumerate(((q_ref, qs), (og_ref, gs))):
            pltpu.make_async_copy(
                wide.at[:, pl.ds(head * hd, hd)], packed.at[pl.ds(head * tok, tok), :], local_sem.at[2 + i]
            ).start()
    p_rows_copy = pltpu.make_async_copy(
        p_ref.at[pl.ds(pl.multiple_of(c * out_rows, out_rows), out_rows), :], p_own, local_sem.at[7]
    )
    p_rows_copy.start()
    pl.semaphore_wait(barrier, chips - 1 + half_ctx)

    place = c // 2

    def peer(step):
        return lax.rem(place + step, half_ctx) * 2 + core

    def source_of(step):
        return lax.rem(place + half_ctx - step, half_ctx) * 2 + core

    def kvs_copies(slot, to, sem):
        return [
            remote(buf.at[slot], buf.at[slot], kvs_send.at[i, sem], kvs_recv.at[i, slot], (d, to))
            for i, buf in enumerate((seg_all, kall, vall))
        ]

    pltpu.make_async_copy(k_ref, kall.at[c], local_sem.at[4]).wait()
    pltpu.make_async_copy(v_ref, vall.at[c], local_sem.at[5]).wait()

    for step in range(1, half_ctx):
        for copy in kvs_copies(c, peer(step), step):
            copy.start()
    for copy in kvs_copies(c, other, 0):
        copy.start()

    chunk_rows = (wide_four + wide_two) // 2

    def p_copy(index, way, device_dp, chunk):
        piece = pall.at[index, pl.ds(chunk * chunk_rows, chunk_rows), :]
        return remote(
            piece, piece, p_send.at[way, index, chunk], p_recv.at[index, chunk], (device_dp, c)
        )

    def pass_on(index, chunk, right, left):
        if right:

            @pl.when(line + 1 < lines)
            def _():
                p_copy(index, 0, d + 2, chunk).start()

        if left:

            @pl.when(line > 0)
            def _():
                p_copy(index, 1, d - 2, chunk).start()

        p_copy(index, 2, mate, chunk).start()

    pltpu.make_async_copy(pall.at[d], pall.at[d], local_sem.at[6]).wait()
    for chunk in range(2):
        pass_on(d, chunk, True, True)

    def member(step):
        return lax.rem(spot + step, members)

    def four_copy(step, index):
        return remote(
            f_ref.at[:, four_at(index, member(step))],
            f4.at[spot, :, four_to(index)],
            mem_send.at[0, step],
            mem_recv.at[0, spot],
            (d, base + member(step)),
        )

    def p_arrived(index, chunk):
        p_copy(index, 2, mate, chunk).wait_recv()

    def project(index):
        cols = pl.ds(pl.multiple_of(index * wide_two, 128), wide_two)
        piece = pall[index, wide_four : wide_four + wide_two, :]
        gacc[spot] += dot_nn(f2[0, :, cols], piece)
        gacc[near] += dot_nn(f2[1, :, cols], piece)
        if wide_four:
            cols = pl.ds(pl.multiple_of(index * wide_four, 128), wide_four)
            lhs = f4[:, :, cols].reshape(members * tok, wide_four)
            out = dot_nn(lhs, pall[index, 0:wide_four, :])
            gacc[...] += out.reshape(members, tok, out.shape[1])

    def forward(distance):
        src = line - distance
        back = line + distance
        for chunk in range(2):

            @pl.when(src >= 0)
            def _():
                p_arrived(src * 2 + side, chunk)
                pass_on(src * 2 + side, chunk, True, False)

            @pl.when(back < lines)
            def _():
                p_arrived(back * 2 + side, chunk)
                pass_on(back * 2 + side, chunk, False, True)

    def project_line(distance):
        @pl.when(line - distance >= 0)
        def _():
            project((line - distance) * 2 + side)

        @pl.when(line + distance < lines)
        def _():
            project((line + distance) * 2 + side)

    def project_across(distance):
        @pl.when(line - distance >= 0)
        def _():
            index = (line - distance) * 2 + 1 - side
            p_arrived(index, 0)
            p_arrived(index, 1)
            project(index)

        if distance > 0:

            @pl.when(line + distance < lines)
            def _():
                index = (line + distance) * 2 + 1 - side
                p_arrived(index, 0)
                p_arrived(index, 1)
                project(index)

    for step in range(1, half_ctx):
        source = source_of(step)
        for landed, onward in zip(
            kvs_copies(source, other, step), kvs_copies(source, other, half_ctx + step)
        ):
            landed.wait_recv()
            onward.start()
    if wide_four:
        for index in range(n_dp):
            for step in range(1, members):
                four_copy(step, index).start()
    for index in range(n_dp):
        remote(
            f_ref.at[:, two_at(index, 1 - core)],
            f2.at[1, :, two_to(index)],
            one_send.at[0],
            one_recv.at[0],
            (d, other),
        ).start()

    for step in range(half_ctx):
        for copy in kvs_copies(lax.rem(place + step, half_ctx) * 2 + 1 - core, other, 0):
            copy.wait_recv()

    width = group * tok
    starts = jnp.zeros((8, width), F32)
    ones = jnp.ones((8, tok), BF16)
    turn = lax.broadcasted_iota(jnp.int32, (width, tok), 0) - lax.broadcasted_iota(
        jnp.int32, (width, tok), 1
    )
    same = jnp.where(lax.rem(turn + tok, tok) == 0, 1.0, 0.0).astype(BF16)
    own_row = jnp.broadcast_to(seg_row_ref[...], (8, tok)).astype(F32).astype(BF16)
    own_col = dot_nt(same, own_row)[:, 0:1]
    for block in range(n_ctx):
        below = jnp.where(seg_all[block].astype(F32) < own_col, 1.0, 0.0).astype(BF16)
        starts = starts + dot_nt(ones, below)
    first_key = starts[0:1, :].astype(jnp.int32)
    lane = lax.broadcasted_iota(jnp.int32, (1, width), 1)
    query_pos = c * tok + lax.rem(lane, tok)
    key_pos = lax.broadcasted_iota(jnp.int32, (seq, width), 0)

    bias[...] = jnp.where((key_pos <= query_pos) & (key_pos >= first_key), 0.0, -1e30)
    pltpu.make_async_copy(qs, qs, local_sem.at[2]).wait()
    pltpu.make_async_copy(gs, gs, local_sem.at[3]).wait()

    def attend(index):
        at = index * group * tok
        keys = kall[...].reshape(seq, hd)
        vals = vall[...].reshape(seq, hd)
        q_now = qs[at : at + width, :]
        g_now = gs[at : at + width, :]
        scores = dot_nt(keys, q_now) * (scale * math.log2(math.e)) + bias[...]
        top = jnp.max(scores, axis=0, keepdims=True)
        expo = jnp.exp2(scores - top)
        inverse = 1.0 / jnp.sum(expo, axis=0, keepdims=True)
        dprob = dot_nt(vals, g_now)
        probs = expo * inverse
        delta = jnp.sum(probs * dprob, axis=0, keepdims=True)
        dscore = (probs * (dprob - delta)).astype(BF16)
        probs_low = probs.astype(BF16)
        dk = (dot_nn(dscore, q_now) * scale).reshape(n_ctx, tok, hd)
        dv = dot_nn(probs_low, g_now).reshape(n_ctx, tok, hd)
        if index == 0:
            kvacc[:, :, 0:hd] = dk
            kvacc[:, :, hd : 2 * hd] = dv
        else:
            kvacc[:, :, 0:hd] += dk
            kvacc[:, :, hd : 2 * hd] += dv
        dq = (dot_tn(dscore, keys) * scale).astype(BF16)
        for h in range(group):
            head = index * group + h
            qg_ref[:, head * hd : (head + 1) * hd] = dq[h * tok : (h + 1) * tok, :]

    groups = HEADS // group
    for index in range(groups):
        attend(index)
        if index == 0 and lines > 1:
            forward(1)
        if index == groups - 2 and lines > 2:
            forward(2)

    def core_copy(index):
        return remote(
            kvacc.at[index * 2 + 1 - core], kv_in.at[index], rs_send.at[0, index], rs_recv.at[0, index], (d, other)
        )

    def kv_copy(step):
        to = lax.rem(place + step, half_ctx)
        return remote(
            kv_sum.at[to], kv_two.at[place], rs_send.at[1, step], rs_recv.at[1, place], (d, to * 2 + core)
        )

    for index in range(half_ctx):
        core_copy(index).start()
    for index in range(half_ctx):
        core_copy(index).wait_recv()
        kv_sum[index] = kvacc[index * 2 + core] + kv_in[index]
    for step in range(1, half_ctx):
        kv_copy(step).start()
    pltpu.make_async_copy(f2.at[0], f2.at[0], local_sem.at[0]).wait()
    remote(f2.at[1], f2.at[1], one_send.at[0], one_recv.at[0], (d, other)).wait_recv()
    if wide_four:
        pltpu.make_async_copy(f4.at[spot], f4.at[spot], local_sem.at[1]).wait()
        for step in range(1, members):
            source = lax.rem(spot + members - step, members)
            remote(
                f4.at[source], f4.at[source], mem_send.at[0, step], mem_recv.at[0, source], (d, other)
            ).wait_recv()
    gacc[...] = jnp.zeros_like(gacc)
    project(d)
    project_across(0)
    if lines > 1:
        project_line(1)
    if lines > 3:
        forward(3)

    total = kv_sum[place]
    for step in range(1, half_ctx):
        source = lax.rem(place + half_ctx - step, half_ctx)
        remote(
            kv_two.at[source], kv_two.at[source], rs_send.at[1, step], rs_recv.at[1, source], (d, other)
        ).wait_recv()
        total = total + kv_two[source]
    kv_all[spot] = total.astype(BF16)

    far = lax.rem(spot + 2, members)

    def kv_low_copy(slot, to, sem):
        return remote(
            kv_all.at[slot],
            kv_all.at[slot],
            mem_send.at[1, sem],
            mem_recv.at[1, slot],
            (d, base + to),
        )

    if members == 4:
        kv_low_copy(spot, far, 1).start()
    kv_low_copy(spot, near, 0).start()

    for distance in range(1, lines):
        if distance > 3:
            forward(distance)
        if distance > 1:
            project_line(distance)
        project_across(distance)
    if members == 4:
        kv_low_copy(far, near, 2).wait_recv()
        kv_low_copy(far, near, 2).start()
        kv_low_copy(lax.rem(near + 2, members), near, 2).wait_recv()
    kv_low_copy(near, near, 0).wait_recv()

    kv_flat = kv_all[...].reshape(members * tok, 2 * hd)
    high, low = split_two(gacc[...].reshape(members * tok, gacc.shape[2]))
    term = dot_tn(high, kv_flat) + dot_tn(low, kv_flat)
    for index in range(chips):
        for k in range(2):
            at = (index * 2 + k) * rows
            pp[k, index] = term[at : at + rows, :]
    swap = remote(pp.at[1 - core], cx, one_send.at[2], one_recv.at[2], (d, other))
    swap.start()
    swap.wait()
    sb[...] = pp[core] + cx[...]

    def sum_copy(step):
        to = lax.rem(chip + step, chips)
        return remote(
            sb.at[to], rb.at[chip], red_send.at[step], red_recv.at[chip], chip_device(to)
        )

    @pl.loop(1, chips)
    def _(step):
        sum_copy(step).start()

    rb[chip] = sb[chip]

    @pl.loop(1, chips)
    def _(step):
        source = lax.rem(chip + chips - step, chips)
        remote(
            rb.at[source], rb.at[source], red_send.at[step], red_recv.at[source], chip_device(source)
        ).wait_recv()

    projected = jnp.sum(rb[...], axis=0)
    first_new = BETA_ONE * m1_ref[...] + (1.0 - BETA_ONE) * projected
    second_new = BETA_TWO * m2_ref[...] + (1.0 - BETA_TWO) * projected * projected
    count = jnp.full((1, 2 * hd), step_ref[0], jnp.int32)

    def one_less_power(beta):
        power = jnp.ones((1, 2 * hd), F32)
        square = jnp.full((1, 2 * hd), beta, F32)
        for bit in range(31):
            power = jnp.where((count >> bit) & 1 == 1, power * square, power)
            square = square * square
        return 1.0 - power

    bias_first = one_less_power(BETA_ONE)
    bias_second = one_less_power(BETA_TWO)
    m1_out[...] = first_new
    m2_out[...] = second_new
    direction = first_new / bias_first / (jnp.sqrt(second_new / bias_second) + EPSILON)
    dual[core, chip] = direction.astype(dual.dtype)

    def dir_copy(step):
        to = lax.rem(chip + step, chips)
        return remote(
            dual.at[core, chip],
            dual.at[core, chip],
            dir_send.at[step],
            dir_recv.at[chip],
            chip_device(to),
        )

    def dir_pass(index):
        return remote(
            dual.at[core, index],
            dual.at[core, index],
            fwd_send.at[index],
            fwd_recv.at[index],
            (d, other),
        )

    @pl.loop(1, chips)
    def _(step):
        dir_copy(step).start()

    dir_pass(chip).start()

    @pl.loop(1, chips)
    def _(step):
        source = lax.rem(chip + chips - step, chips)
        remote(
            dual.at[core, source],
            dual.at[core, source],
            dir_send.at[step],
            dir_recv.at[source],
            chip_device(source),
        ).wait_recv()
        dir_pass(source).start()

    @pl.loop(0, chips)
    def _(index):
        remote(
            dual.at[1 - core, index],
            dual.at[1 - core, index],
            fwd_send.at[index],
            fwd_recv.at[index],
            (d, other),
        ).wait_recv()

    for index in range(chips):
        at = index * 2 * rows
        dfull[at : at + rows, :] = dual[0, index]
        dfull[at + rows : at + 2 * rows, :] = dual[1, index]
    p_rows_copy.wait()
    p_rows = p_own[...]
    if dfull.dtype == BF16:
        up_ref[...] = dot_nn(p_rows, dfull[...])
    else:
        high, low = split_two(dfull[...])
        up_ref[...] = dot_nn(p_rows, high) + dot_nn(p_rows, low)

    for step in range(half_ctx):
        for copy in kvs_copies(c, other, step):
            copy.wait_send()
        if step > 0:
            for copy in kvs_copies(c, other, half_ctx + step):
                copy.wait_send()
    for step in range(1, half_ctx):
        kv_copy(step).wait_send()
    for index in range(half_ctx):
        core_copy(index).wait_send()
    remote(f2.at[1], f2.at[1], one_send.at[0], one_recv.at[0], (d, other)).wait_send()
    for step in range(1, members):
        kv_low_copy(spot, near, step - 1).wait_send()
        if wide_four:
            remote(
                f4.at[0], f4.at[0], mem_send.at[0, step], mem_recv.at[0, 0], (d, other)
            ).wait_send()

    @pl.loop(0, chips)
    def _(index):
        dir_pass(index).wait_send()

    @pl.loop(1, chips)
    def _(step):
        sum_copy(step).wait_send()
        dir_copy(step).wait_send()

    def sent(index, right, left):
        for chunk in range(2):
            p_copy(index, 2, mate, chunk).wait_send()
            if right:

                @pl.when(line + 1 < lines)
                def _():
                    p_copy(index, 0, d + 2, chunk).wait_send()

            if left:

                @pl.when(line > 0)
                def _():
                    p_copy(index, 1, d - 2, chunk).wait_send()

    sent(d, True, True)
    for distance in range(1, lines):

        @pl.when(line - distance >= 0)
        def _():
            sent((line - distance) * 2 + side, True, False)

        @pl.when(line + distance < lines)
        def _():
            sent((line + distance) * 2 + side, False, True)


def hand_over(*refs):
    ins, outs, held, sems = refs[0:4], refs[4:8], refs[8:12], refs[12]
    load = [pltpu.make_async_copy(x, y, sems.at[0, i]) for i, (x, y) in enumerate(zip(ins, held))]
    store = [pltpu.make_async_copy(x, y, sems.at[1, i]) for i, (x, y) in enumerate(zip(held, outs))]
    for copy in load:
        copy.start()
    for first, then in zip(load, store):
        first.wait()
        then.start()
    for copy in store:
        copy.wait()


def shards(
    n_dp,
    n_ctx,
    queries,
    keys,
    values,
    out_grad,
    segments,
    features,
    projector,
    first_moment,
    second_moment,
    adam_step,
):
    tok, hd = keys.shape[1], keys.shape[2]
    width = features.shape[2]
    slab, rank = projector.shape
    rows, kvw = first_moment.shape
    chips = n_dp * n_ctx // 2
    group = 2 if n_ctx * tok <= 1024 else 1
    members, wide_four = (4, slab // 8) if slab % 1024 == 0 and n_ctx % 4 == 0 else (2, 0)
    wide_two = (slab - members * wide_four) // 2
    dir_type = BF16 if rows % 16 == 0 else F32
    vmem = pl.BlockSpec(memory_space=pltpu.VMEM)
    hbm = pl.BlockSpec(memory_space=pl.ANY)
    dma = pltpu.SemaphoreType.DMA
    results = pl.pallas_call(
        functools.partial(body, n_dp, n_ctx, group, members, wide_four),
        out_shape=(
            jax.ShapeDtypeStruct((tok, HEADS * hd), BF16),
            jax.ShapeDtypeStruct((width // (n_dp * n_ctx), kvw), F32),
            jax.ShapeDtypeStruct((rows, kvw), F32),
            jax.ShapeDtypeStruct((rows, kvw), F32),
        ),
        in_specs=[hbm] * 4 + [vmem] + [hbm] * 2 + [vmem] * 2 + [pl.BlockSpec(memory_space=pltpu.SMEM)],
        out_specs=[vmem] * 4,
        scratch_shapes=[
            pltpu.VMEM((HEADS * tok, hd), BF16),
            pltpu.VMEM((HEADS * tok, hd), BF16),
            pltpu.VMEM((n_ctx, tok, hd), BF16),
            pltpu.VMEM((n_ctx, tok, hd), BF16),
            pltpu.VMEM((n_ctx, 1, tok), jnp.int32),
            pltpu.VMEM((n_ctx, tok, kvw), F32),
            pltpu.VMEM((n_ctx // 2, tok, kvw), F32),
            pltpu.VMEM((n_ctx // 2, tok, kvw), F32),
            pltpu.VMEM((n_ctx // 2, tok, kvw), F32),
            pltpu.VMEM((members, tok, kvw), BF16),
            pltpu.VMEM((n_dp, wide_four + wide_two, rank), BF16),
            pltpu.VMEM((2, tok, n_dp * wide_two), BF16),
            pltpu.VMEM((members, tok, n_dp * max(wide_four, 128)), BF16),
            pltpu.VMEM((members, tok, rank), F32),
            pltpu.VMEM((2, chips, rows, kvw), F32),
            pltpu.VMEM((chips, rows, kvw), F32),
            pltpu.VMEM((chips, rows, kvw), F32),
            pltpu.VMEM((chips, rows, kvw), F32),
            pltpu.VMEM((2, chips, rows, kvw), dir_type),
            pltpu.VMEM((rank, kvw), dir_type),
            pltpu.VMEM((slab // n_ctx, rank), BF16),
            pltpu.VMEM((n_ctx * tok, group * tok), F32),
            dma((3, n_ctx)),
            dma((3, n_ctx)),
            dma((2, n_ctx // 2)),
            dma((2, n_ctx // 2)),
            dma((3, n_dp, 2)),
            dma((n_dp, 2)),
            dma((4,)),
            dma((4,)),
            dma((8,)),
            dma((chips,)),
            dma((chips,)),
            dma((chips,)),
            dma((chips,)),
            dma((chips,)),
            dma((chips,)),
            dma((2, members)),
            dma((2, members)),
        ],
        compiler_params=pltpu.CompilerParams(
            collective_id=0, has_side_effects=True, vmem_limit_bytes=56 * 2**20
        ),
    )(
        queries[0],
        keys[0],
        values[0],
        out_grad[0],
        segments,
        features[0],
        projector,
        first_moment,
        second_moment,
        adam_step,
    )
    query_grad, update, first_new, second_new = pl.pallas_call(
        hand_over,
        out_shape=tuple(jax.ShapeDtypeStruct(r.shape, r.dtype) for r in results),
        in_specs=[hbm] * 4,
        out_specs=[hbm] * 4,
        scratch_shapes=[pltpu.VMEM(r.shape, r.dtype) for r in results] + [dma((2, 4))],
        compiler_params=pltpu.CompilerParams(vmem_limit_bytes=60 * 2**20),
    )(*results)
    return (query_grad[None], update, first_new, second_new)


def solution(mesh):
    in_specs = (
        P("dp", "ctx", None),
        P("dp", "ctx", None),
        P("dp", "ctx", None),
        P("dp", "ctx", None),
        P("dp", "ctx"),
        P("dp", "ctx", None),
        P("dp", None),
        P(("dp", "ctx"), None),
        P(("dp", "ctx"), None),
        P(),
    )
    out_specs = (
        P("dp", "ctx", None),
        P(("dp", "ctx"), None),
        P(("dp", "ctx"), None),
        P(("dp", "ctx"), None),
    )
    fn = functools.partial(shards, mesh.shape["dp"], mesh.shape["ctx"])
    return jax.shard_map(fn, mesh=mesh, in_specs=in_specs, out_specs=out_specs, check_vma=False)
```
